32 devices in a mesh: band: 4 (over y, x), set: 8 (over z, core).
Axes of the slice: x: 2, y: 2, z: 4, core: 2. Of those that a mesh axis runs over, the one named last changes fastest.
Arguments:
- grid: float32 [8, 5152, 128], P('band', 'set'), may hold values from -6 to 6
- row_points: int32 [8], P('band'), may hold values from 20 to 5136, as said below
- legendre: bfloat16 [640, 8, 1408], P('set'), may hold values from -1.5 to 1.5
Outputs:
- spectra: float32 [640, 1408, 128], P('set', 'band')
The draws below stay inside these ranges and needn't reach their ends.
Inputs may be any that keep to these rules, and one draw needn't show every extreme that they name: row_points[r] is 4 j + 20 for some row j of the model grid with r * (160) <= j < (r + 1) * 160; the last row has 5136 points.
All inputs are finite; a program needn't handle non-finite values.
Results may differ from the reference program's by a relative error of at most 0.0029.
Values may be sent and summed in bfloat16 or wider, within the bound.
No kernel may reach another device: no remote copies, remote signals or barrier semaphores. Data moves between devices by JAX's collectives and lax.ppermute only.
A program may use at most 64 MiB of HBM per device.

```python
import math
import jax
import jax.numpy as jnp
from jax import lax

TRUNC = 1279
COLS = 64
WAVES = 1280
PAIRS = 640
NPAD = 1408
LATS = 8
CAP = 5152


def draw_row_points(key, part):
    row_ids = jnp.arange(LATS, dtype=jnp.int32)
    stride = WAVES // LATS
    offsets = jax.random.randint(key, (LATS,), 0, stride, dtype=jnp.int32)
    latitude = jnp.where(row_ids == LATS - 1, WAVES - 1, row_ids * stride + offsets)
    return (4 * latitude + 20).astype(jnp.int32)


def levels(stream_key, extent, pieces, least, largest):
    gain = 1.0
    for dim, parts in pieces:
        steps = jax.random.uniform(jax.random.fold_in(jax.random.fold_in(stream_key, 6), dim), (parts,), jnp.float32, least / len(pieces), largest / len(pieces))
        gain = gain * jnp.repeat(jnp.exp(steps), extent[dim] // parts).reshape((-1,) + (1,) * (len(extent) - 1 - dim))
    return gain


def normal_values(stream_key, dims, deviation, most, pieces=(), held_as=jnp.bfloat16):
    gain = levels(stream_key, dims, pieces, -0.22, 0.18) if pieces else 1.0
    entries = jax.random.normal(stream_key, dims, jnp.float32) * deviation * gain
    return jnp.minimum(jnp.maximum(entries, -most), most).astype(held_as)


def setup_inputs(seed: int = 0) -> dict:
    splits = jax.random.split(jax.random.key(seed), 4)
    return {
        "grid": normal_values(splits[0], (LATS, CAP, 2 * COLS), 1.0, 6.0, ((0, 4), (1, 8)), jnp.float32),
        "row_points": draw_row_points(jax.random.fold_in(splits[3], 71), 0),
        "legendre": normal_values(splits[2], (PAIRS, LATS, NPAD), (2 * LATS) ** -0.5, 1.5, ((0, 8),)),
    }


def reference(grid, row_points, legendre):
    waves = TRUNC + 1
    point_ids = jnp.arange(CAP, dtype=jnp.int32)
    wave_ids = jnp.arange(waves, dtype=jnp.int32)

    def row_transform(item):
        row_block, length = item
        residue = point_ids[:, None] * wave_ids[None, :] % length
        length_float = length.astype(jnp.float32)
        phases = residue.astype(jnp.float32) * (2.0 * math.pi / length_float)
        usable = (point_ids[:, None] < length) & (wave_ids[None, :] <= (length - 1) // 2)
        row_scale = lax.rsqrt(length_float)
        cosine_part = jnp.where(usable, jnp.cos(phases) * row_scale, 0.0)
        sine_part = jnp.where(usable, -jnp.sin(phases) * row_scale, 0.0)
        table = jnp.stack([cosine_part, sine_part], axis=1)
        values = row_block.reshape(CAP, 2, COLS)
        fourier = jnp.einsum('qhc,qem->mhec', values, table, precision=lax.Precision.HIGHEST)
        halves = jnp.stack([fourier[:, 0] + fourier[:, 1], fourier[:, 0] - fourier[:, 1]], axis=1)
        return halves.reshape(waves, 2, 2 * COLS).astype(jnp.bfloat16)
    halves = lax.map(row_transform, (grid, row_points))
    slot_ids = jnp.arange(NPAD, dtype=jnp.int32)
    class_ids = jnp.arange(4, dtype=jnp.int32)

    def pair_spectra(pair_id):
        legend_rows = legendre[pair_id].astype(jnp.float32)
        side_one = lax.dynamic_index_in_dim(halves, pair_id, 1, keepdims=False)
        side_two = lax.dynamic_index_in_dim(halves, TRUNC - pair_id, 1, keepdims=False)
        sources = jnp.concatenate([side_one, side_two], axis=1).astype(jnp.float32)
        products = jnp.einsum('rk,rjc->kjc', legend_rows, sources)
        is_first = slot_ids <= TRUNC - pair_id
        parity = jnp.where(is_first, slot_ids % 2, (slot_ids - 1 - TRUNC + pair_id) % 2)
        selector = jnp.where(is_first, 0, 2) + parity
        weights = (selector[:, None] == class_ids[None, :]).astype(jnp.float32)
        return lax.optimization_barrier(jnp.sum(products * weights[:, :, None], axis=1))
    return lax.map(pair_spectra, jnp.arange(PAIRS, dtype=jnp.int32))
```

```python
import functools
import math

import jax
import jax.numpy as jnp
from jax import lax
from jax.experimental import pallas as pl
from jax.experimental.pallas import tpu as pltpu
from jax.sharding import PartitionSpec as P

TRUNC = 1279
GROUP = 8
F32 = jnp.float32
BF16 = jnp.bfloat16
WIRE = jnp.float16


def round_up(value, step):
    return -(-value // step) * step


def unit_circle(multiplier, point, length, inverse):
    product = (multiplier * point).astype(F32)
    residue = product - jnp.floor(product * inverse + 0.5) * length
    quarters = 4.0 * residue * inverse
    turn = jnp.floor(quarters + 0.5)
    angle = (quarters - turn) * (0.5 * math.pi)
    square = angle * angle
    sine = angle * (1.0 + square * (-1 / 6 + square * (1 / 120 + square * (-1 / 5040 + square / 362880))))
    cosine = 1.0 + square * (-0.5 + square * (1 / 24 + square * (-1 / 720 + square / 40320)))
    quadrant = turn.astype(jnp.int32) & 3
    odd = (quadrant & 1) == 1
    real = jnp.where(odd, sine, cosine)
    imag = jnp.where(odd, cosine, sine)
    real = jnp.where((quadrant == 1) | (quadrant == 2), -real, real)
    imag = jnp.where(quadrant >= 2, imag, -imag)
    return real, imag


def rotate(a, b):
    return a[0] * b[0] - a[1] * b[1], a[0] * b[1] + a[1] * b[0]


def split(values):
    high = values.astype(BF16)
    return high, (values - high.astype(F32)).astype(BF16)


def fourier_kernel(groups, first_group, peers, seg, points, info, mine, theirs, *refs):
    outs = refs[:peers]
    values, factor, table, sums = refs[peers:]
    rows = mine.shape[0]
    width = mine.shape[2]
    depth = values.shape[0]
    lane = lax.broadcasted_iota(jnp.int32, (1, width), 1)
    north = lane < width // 2
    slot = lax.broadcasted_iota(jnp.int32, (1, depth), 1)
    point = jnp.where(slot < seg, info[0] + slot, info[1] + slot - seg)
    sub = lax.broadcasted_iota(jnp.int32, (GROUP, 1), 0)
    tiles = peers * groups * 2
    for r in range(rows):
        length_int = info[2 + r]
        length = length_int.astype(F32)
        inverse = 1.0 / length
        scale = lax.rsqrt(jnp.full((1, width), length, F32))
        values[...] = jnp.zeros(values.shape, BF16)
        for half, block in enumerate((mine, theirs)):
            raw = block[r]
            where = info[half] + lax.broadcasted_iota(jnp.int32, (points, 1), 0)
            folded = pltpu.roll(raw, width // 2, 1) + jnp.where(north, raw, -raw)
            folded = jnp.where(where < length_int, folded * scale, 0.0)
            high, low = split(folded)
            values[half * seg:half * seg + points, :width] = high
            values[half * seg:half * seg + points, width:] = low
        near = unit_circle(sub, point, length, inverse)
        last = unit_circle(TRUNC, point, length, inverse)
        for peer in range(peers):
            for g in range(groups):
                base = info[2 + rows + peer] + (first_group + g) * GROUP
                index = peer * groups + g
                real, imag = unit_circle(base, point, length, inverse)
                factor[0, index:index + 1, :] = real
                factor[1, index:index + 1, :] = imag

        def fill(index, carry):
            base = factor[0, pl.ds(index, 1), :], factor[1, pl.ds(index, 1), :]
            first = rotate(base, near)
            second = rotate(last, (first[0], -first[1]))
            block = jnp.concatenate([*first, *second], axis=0)
            high, low = split(block)
            start = pl.multiple_of(index * 4 * GROUP, 4 * GROUP)
            table[0, pl.ds(start, 4 * GROUP), :] = high
            table[1, pl.ds(start, 4 * GROUP), :] = low
            return carry

        lax.fori_loop(0, peers * groups, fill, 0)
        wide = jnp.dot(table[0], values[...], preferred_element_type=F32)
        narrow = jnp.dot(table[1], values[:, :width], preferred_element_type=F32)
        sums[r] = wide[:, :width] + wide[:, width:] + narrow
    for peer in range(peers):
        for g in range(groups):
            base = info[2 + rows + peer] + (first_group + g) * GROUP
            for side in range(2):
                wave = base + sub
                wave = TRUNC - wave if side else wave
                at = ((peer * groups + g) * 2 + side) * 2 * GROUP
                for r in range(rows):
                    real = sums[r, at:at + GROUP, :]
                    imag = sums[r, at + GROUP:at + 2 * GROUP, :]
                    usable = wave <= (info[2 + r] - 1) // 2
                    even = jnp.where(north, real, pltpu.roll(imag, width // 2, 1))
                    odd = jnp.where(north, pltpu.roll(real, width // 2, 1), imag)
                    for parity, block in enumerate((even, odd)):
                        to = (((g * 2 + side) * 2 + parity) * rows + r) * GROUP
                        outs[peer][to:to + GROUP, :] = jnp.where(usable, block, 0.0)


def fourier_sums(info, mine, theirs, groups, first_group, peers):
    rows, points, width = mine.shape
    seg = round_up(points, 16)
    depth = round_up(2 * seg, 128)
    out_rows = groups * 4 * rows * GROUP
    tall = peers * groups * 4 * GROUP
    vmem = pl.BlockSpec(memory_space=pltpu.VMEM)
    return pl.pallas_call(
        functools.partial(fourier_kernel, groups, first_group, peers, seg, points),
        out_shape=[jax.ShapeDtypeStruct((out_rows, width), F32)] * peers,
        in_specs=[pl.BlockSpec(memory_space=pltpu.SMEM), vmem, vmem],
        out_specs=[vmem] * peers,
        scratch_shapes=[
            pltpu.VMEM((depth, 2 * width), BF16),
            pltpu.VMEM((2, round_up(peers * groups, 8), depth), F32),
            pltpu.VMEM((2, tall, depth), BF16),
            pltpu.VMEM((rows, tall, width), F32),
        ],
        compiler_params=pltpu.CompilerParams(vmem_limit_bytes=48 * 2**20),
        name="fourier_sums",
    )(info, mine, theirs)


def weights_kernel(pair_count, rows, bands, info, legend, out):
    group = pl.program_id(0)
    total = rows * bands
    slots = legend.shape[2]
    wide = out.shape[2]
    held = legend[...].astype(F32)
    pair = group * GROUP + lax.broadcasted_iota(jnp.int32, (GROUP, 1, 1), 0)
    held = jnp.where(pair < pair_count, held, 0.0).reshape(GROUP * total, slots).astype(BF16)
    source = lax.broadcasted_iota(jnp.int32, (GROUP * total, 1), 0)
    lane = lax.broadcasted_iota(jnp.int32, (1, wide), 1)
    member = lane % GROUP
    row = lane // GROUP % rows
    parity = lane // (GROUP * rows) % 2
    side = lane // (GROUP * rows * 2) % 2
    band = (lane // (GROUP * rows * 4)) ^ info[0]
    spread = (source == member * total + band * rows + row).astype(F32).astype(BF16)
    moved = lax.dot_general(held, spread, (((0,), (0,)), ((), ())), preferred_element_type=F32)
    slot = info[1] + lax.broadcasted_iota(jnp.int32, (slots, 1), 0)
    first = TRUNC - (info[2] + group * GROUP + member)
    is_first = slot <= first
    count = jnp.where(is_first, slot, slot - 1 - first)
    match = ((count & 1) == parity) & (is_first == (side == 0))
    out[0] = jnp.where(match, moved, 0.0).astype(BF16)


def spread_weights(info, legend, rows, bands):
    pair_count, total, slots = legend.shape
    groups = pl.cdiv(pair_count, GROUP)
    wide = bands * 4 * rows * GROUP
    return pl.pallas_call(
        functools.partial(weights_kernel, pair_count, rows, bands),
        grid=(groups,),
        out_shape=jax.ShapeDtypeStruct((groups, slots, wide), BF16),
        in_specs=[
            pl.BlockSpec(memory_space=pltpu.SMEM),
            pl.BlockSpec((GROUP, total, slots), lambda g: (g, 0, 0)),
        ],
        out_specs=pl.BlockSpec((1, slots, wide), lambda g: (g, 0, 0)),
        compiler_params=pltpu.CompilerParams(vmem_limit_bytes=48 * 2**20),
        name="spread_weights",
    )(info, legend)


def spectra_kernel(bands, weights, *refs):
    held = refs[:bands]
    out = refs[-1]
    width = held[0].shape[1]
    stacked = jnp.concatenate([ref[...] for ref in held], axis=0)
    member = lax.broadcasted_iota(jnp.int32, stacked.shape, 0) % GROUP
    for at in range(0, GROUP, 2):
        pairs = [stacked * (member == at + i).astype(F32).astype(BF16) for i in range(2)]
        product = jnp.dot(weights[0], jnp.concatenate(pairs, axis=1), preferred_element_type=F32)
        out[at] = product[:, :width]
        out[at + 1] = product[:, width:]


def spectra_part(weights, held, out, pair_count, first_group):
    bands = len(held)
    width = held[0].shape[1]
    slots, wide = weights.shape[1:]
    block = wide // bands
    groups = held[0].shape[0] // block
    previous = [] if out is None else [out]
    return pl.pallas_call(
        functools.partial(spectra_kernel, bands),
        grid=(groups,),
        out_shape=jax.ShapeDtypeStruct((pair_count, slots, width), F32),
        in_specs=[pl.BlockSpec((1, slots, wide), lambda g: (first_group + g, 0, 0))]
        + [pl.BlockSpec((block, width), lambda g: (g, 0))] * bands
        + [pl.BlockSpec(memory_space=pl.ANY)] * len(previous),
        out_specs=pl.BlockSpec((GROUP, slots, width), lambda g: (first_group + g, 0, 0)),
        input_output_aliases={1 + bands: 0} if previous else {},
        compiler_params=pltpu.CompilerParams(vmem_limit_bytes=48 * 2**20),
        name="spectra_part",
    )(weights, *held, *previous)


def swap(axis, size, step):
    return [(i, i ^ step) for i in range(size)]


def shards(grid, row_points, legendre):
    set_index = lax.axis_index("set")
    set_size = lax.axis_size("set")
    band_index = lax.axis_index("band")
    band_size = lax.axis_size("band")
    rows, points, width = grid.shape
    pair_count = legendre.shape[0]
    slots = legendre.shape[2] // band_size
    peers = set_size // 2
    theirs = lax.ppermute(grid, "set", swap("set", set_size, 1))
    steps = jnp.arange(peers, dtype=jnp.int32) * 2
    places = jnp.stack([set_index * points, (set_index ^ 1) * points])
    info = jnp.concatenate([places, row_points, (set_index ^ steps) * pair_count]).astype(jnp.int32)
    legend = lax.dynamic_slice_in_dim(legendre, band_index * slots, slots, 2)
    place = jnp.stack([band_index, band_index * slots, set_index * pair_count]).astype(jnp.int32)
    weights = spread_weights(place, legend, rows, band_size)
    all_groups = pl.cdiv(pair_count, GROUP)
    cut = (all_groups + 1) // 2
    out = None
    for first_group, groups in ((0, cut), (cut, all_groups - cut)):
        parts = fourier_sums(info, grid, theirs, groups, first_group, peers)
        total = parts[0]
        for k in range(1, peers):
            arrived = lax.ppermute(parts[k].astype(WIRE), "set", swap("set", set_size, 2 * k))
            total = total + arrived.astype(F32)
        rounded = total.astype(BF16)
        held = [rounded]
        for k in range(1, band_size):
            held.append(lax.ppermute(rounded, "band", swap("band", band_size, k)))
        out = spectra_part(weights, held, out, pair_count, first_group)
    return out


def solution(mesh):
    return jax.shard_map(
        shards,
        mesh=mesh,
        in_specs=(P("band", "set", None), P("band"), P("set", None, None)),
        out_specs=P("set", "band", None),
        check_vma=False,
    )
```

```python
import functools
import math

import jax
import jax.numpy as jnp
from jax import lax
from jax.experimental import pallas as pl
from jax.experimental.pallas import tpu as pltpu
from jax.sharding import PartitionSpec as P

TRUNC = 1279
GROUP = 8
F32 = jnp.float32
BF16 = jnp.bfloat16
WIRE = jnp.float16


def round_up(value, step):
    return -(-value // step) * step


def unit_circle(multiplier, point, length, inverse):
    product = (multiplier * point).astype(F32)
    residue = product - jnp.floor(product * inverse + 0.5) * length
    quarters = 4.0 * residue * inverse
    turn = jnp.floor(quarters + 0.5)
    angle = (quarters - turn) * (0.5 * math.pi)
    square = angle * angle
    sine = angle * (1.0 + square * (-1 / 6 + square * (1 / 120 + square * (-1 / 5040 + square / 362880))))
    cosine = 1.0 + square * (-0.5 + square * (1 / 24 + square * (-1 / 720 + square / 40320)))
    quadrant = turn.astype(jnp.int32) & 3
    odd = (quadrant & 1) == 1
    real = jnp.where(odd, sine, cosine)
    imag = jnp.where(odd, cosine, sine)
    real = jnp.where((quadrant == 1) | (quadrant == 2), -real, real)
    imag = jnp.where(quadrant >= 2, imag, -imag)
    return real, imag


def rotate(a, b):
    return a[0] * b[0] - a[1] * b[1], a[0] * b[1] + a[1] * b[0]


def split(values):
    high = values.astype(BF16)
    return high, (values - high.astype(F32)).astype(BF16)


def prepare_values(raw, start, length, length_int):
    width = raw.shape[1]
    lane = lax.broadcasted_iota(jnp.int32, (1, width), 1)
    where = start + lax.broadcasted_iota(jnp.int32, (raw.shape[0], 1), 0)
    folded = pltpu.roll(raw, width // 2, 1) + jnp.where(lane < width // 2, raw, -raw)
    scale = lax.rsqrt(jnp.full((1, width), length, F32))
    return split(jnp.where(where < length_int, folded * scale, 0.0))


def store_values(out, r, raw, start, length_int):
    points, width = raw.shape
    out[r, :points, :width], out[r, :points, width:] = prepare_values(raw, start, length_int.astype(F32), length_int)
    out[r, points:, :] = jnp.zeros((out.shape[1] - points, 2 * width), BF16)


def row_of(block, r, rows):
    return block[pl.ds(r, block.shape[0] // rows, stride=rows), :]


def prepare_kernel(peers, pair_count, points, row_points, mine, values, factor):
    rows, _, tall, depth = factor.shape
    held = round_up(pl.cdiv(pair_count, GROUP), GROUP)
    set_index = lax.axis_index("set")
    start = set_index * points
    beside = (set_index ^ 1) * points - start
    slot = lax.broadcasted_iota(jnp.int32, (1, depth), 1)
    point = jnp.where(slot < values.shape[1], start + slot, beside)
    heads = round_up(peers + 1, GROUP)
    sub = lax.broadcasted_iota(jnp.int32, (GROUP + heads + held, 1), 0)
    order = sub - GROUP
    head = jnp.where(order < peers, (set_index ^ (2 * order)) * pair_count, TRUNC)
    multiplier = jnp.where(sub < GROUP, sub, jnp.where(order < heads, head, (order - heads) * GROUP))
    for r in range(rows):
        length = row_points[r].astype(F32)
        real, imag = unit_circle(multiplier, point, length, 1.0 / length)
        factor[r, 0, :GROUP, :] = real[:GROUP]
        factor[r, 1, :GROUP, :] = imag[:GROUP]
        last = GROUP + peers
        factor[r, 0, GROUP:2 * GROUP, :] = jnp.broadcast_to(real[last:last + 1], (GROUP, depth))
        factor[r, 1, GROUP:2 * GROUP, :] = jnp.broadcast_to(imag[last:last + 1], (GROUP, depth))
        tail = real[GROUP + heads:], imag[GROUP + heads:]
        for peer in range(peers):
            at = GROUP + peer
            base = rotate((real[at:at + 1], imag[at:at + 1]), tail)
            to = 2 * GROUP + peer * held
            factor[r, 0, to:to + held, :] = base[0]
            factor[r, 1, to:to + held, :] = base[1]
        store_values(values, r, row_of(mine, r, rows), start, row_points[r])


def prepare(row_points, mine, peers, pair_count):
    rows = row_points.shape[0]
    points, width = mine.shape[0] // rows, mine.shape[1]
    depth = round_up(points, 128)
    tall = 2 * GROUP + peers * round_up(pl.cdiv(pair_count, GROUP), GROUP)
    vmem = pl.BlockSpec(memory_space=pltpu.VMEM)
    return pl.pallas_call(
        functools.partial(prepare_kernel, peers, pair_count, points),
        out_shape=[
            jax.ShapeDtypeStruct((rows, depth, 2 * width), BF16),
            jax.ShapeDtypeStruct((rows, 2, tall, depth + 128), F32),
        ],
        in_specs=[pl.BlockSpec(memory_space=pltpu.SMEM), vmem],
        out_specs=[vmem, vmem],
        compiler_params=pltpu.CompilerParams(vmem_limit_bytes=48 * 2**20),
        name="prepare",
    )(row_points, mine)


def fourier_kernel(groups, first_group, peers, pair_count, fresh, row_points, mine, theirs, factor, *refs):
    outs = refs[:peers]
    table, sums, twist = refs[-3:]
    rows, depth, double = mine.shape
    width = double // 2
    held = round_up(pl.cdiv(pair_count, GROUP), GROUP)
    set_index = lax.axis_index("set")
    if fresh:
        values = refs[peers]
        points = theirs.shape[0] // rows
        for r in range(rows):
            store_values(values, r, row_of(theirs, r, rows), (set_index ^ 1) * points, row_points[r])
    else:
        values = theirs
    lane = lax.broadcasted_iota(jnp.int32, (1, width), 1)
    north = lane < width // 2
    sub = lax.broadcasted_iota(jnp.int32, (GROUP, 1), 0)
    for r in range(rows):

        def fill(index, carry):
            at = 2 * GROUP + index // groups * held + first_group + index % groups
            base = factor[r, 0, pl.ds(at, 1), :], factor[r, 1, pl.ds(at, 1), :]
            first = rotate(base, (factor[r, 0, :GROUP, :], factor[r, 1, :GROUP, :]))
            last = factor[r, 0, GROUP:2 * GROUP, :], factor[r, 1, GROUP:2 * GROUP, :]
            second = rotate(last, (first[0], -first[1]))
            block = jnp.concatenate([*first, *second], axis=0)
            high, low = split(block[:, :depth])
            start = pl.multiple_of(index * 4 * GROUP, 4 * GROUP)
            table[0, pl.ds(start, 4 * GROUP), :] = high
            table[1, pl.ds(start, 4 * GROUP), :] = low
            twist[r, pl.ds(start, 4 * GROUP), :] = block[:, depth:]
            return carry

        lax.fori_loop(0, peers * groups, fill, 0, unroll=2)
        own = jnp.dot(table[0], mine[r], preferred_element_type=F32)
        other = jnp.dot(table[0], values[r], preferred_element_type=F32)
        both = jnp.concatenate([mine[r, :, :width], values[r, :, :width]], axis=1)
        rest = jnp.dot(table[1], both, preferred_element_type=F32)
        sums[r, :, :width] = own[:, :width] + own[:, width:] + rest[:, :width]
        sums[r, :, width:] = other[:, :width] + other[:, width:] + rest[:, width:]
    for peer in range(peers):
        for g in range(groups):
            base = (set_index ^ (2 * peer)) * pair_count + (first_group + g) * GROUP
            for side in range(2):
                wave = base + sub
                wave = TRUNC - wave if side else wave
                at = ((peer * groups + g) * 2 + side) * 2 * GROUP
                for r in range(rows):
                    turn = twist[r, at:at + GROUP, :], twist[r, at + GROUP:at + 2 * GROUP, :]
                    far = sums[r, at:at + GROUP, width:], sums[r, at + GROUP:at + 2 * GROUP, width:]
                    far = rotate(turn, far)
                    real = sums[r, at:at + GROUP, :width] + far[0]
                    imag = sums[r, at + GROUP:at + 2 * GROUP, :width] + far[1]
                    usable = wave <= (row_points[r] - 1) // 2
                    even = jnp.where(north, real, pltpu.roll(imag, width // 2, 1))
                    odd = jnp.where(north, pltpu.roll(real, width // 2, 1), imag)
                    for parity, block in enumerate((even, odd)):
                        to = (((g * 2 + side) * 2 + parity) * rows + r) * GROUP
                        outs[peer][to:to + GROUP, :] = jnp.where(usable, block, 0.0)


def fourier_sums(row_points, mine, theirs, factor, groups, first_group, peers, pair_count):
    rows, depth, double = mine.shape
    width = double // 2
    fresh = theirs.ndim == 2
    out_rows = groups * 4 * rows * GROUP
    tall = peers * groups * 4 * GROUP
    vmem = pl.BlockSpec(memory_space=pltpu.VMEM)
    out_shape = [jax.ShapeDtypeStruct((out_rows, width), F32)] * peers
    out_shape += [jax.ShapeDtypeStruct(mine.shape, BF16)] if fresh else []
    return pl.pallas_call(
        functools.partial(fourier_kernel, groups, first_group, peers, pair_count, fresh),
        out_shape=out_shape,
        in_specs=[pl.BlockSpec(memory_space=pltpu.SMEM), vmem, vmem, vmem],
        out_specs=[vmem] * len(out_shape),
        scratch_shapes=[
            pltpu.VMEM((2, tall, depth), BF16),
            pltpu.VMEM((rows, tall, double), F32),
            pltpu.VMEM((rows, tall, 128), F32),
        ],
        compiler_params=pltpu.CompilerParams(vmem_limit_bytes=48 * 2**20),
        name="fourier_sums",
    )(row_points, mine, theirs, factor)


def weights_kernel(rows, bands, legend, out):
    pair_count, total, slots = legend.shape
    wide = out.shape[2]
    band_index = lax.axis_index("band")
    first_pair = lax.axis_index("set") * pair_count
    source = lax.broadcasted_iota(jnp.int32, (GROUP * total, 1), 0)
    lane = lax.broadcasted_iota(jnp.int32, (1, wide), 1)
    member = lane % GROUP
    row = lane // GROUP % rows
    parity = lane // (GROUP * rows) % 2
    side = lane // (GROUP * rows * 2) % 2
    band = (lane // (GROUP * rows * 4)) ^ band_index
    spread = (source == member * total + band * rows + row).astype(F32).astype(BF16)
    slot = band_index * slots + lax.broadcasted_iota(jnp.int32, (slots, 1), 0)
    for group in range(out.shape[0]):
        count = min(GROUP, pair_count - group * GROUP)
        held = legend[group * GROUP:group * GROUP + count].astype(F32).reshape(count * total, slots)
        if count < GROUP:
            held = jnp.concatenate([held, jnp.zeros(((GROUP - count) * total, slots), F32)], axis=0)
        moved = lax.dot_general(
            held.astype(BF16), spread, (((0,), (0,)), ((), ())), preferred_element_type=F32
        )
        first = TRUNC - (first_pair + group * GROUP + member)
        start = jnp.where(side == 0, 0, first + 1)
        sign = 1 - 2 * side
        match = (((slot - start) & 1) == parity) & (sign * slot <= sign * first - side)
        out[group] = jnp.where(match, moved, 0.0).astype(BF16)


def spread_weights(legend, rows, bands):
    pair_count, total, slots = legend.shape
    groups = pl.cdiv(pair_count, GROUP)
    vmem = pl.BlockSpec(memory_space=pltpu.VMEM)
    return pl.pallas_call(
        functools.partial(weights_kernel, rows, bands),
        out_shape=jax.ShapeDtypeStruct((groups, slots, bands * 4 * rows * GROUP), BF16),
        in_specs=[vmem],
        out_specs=vmem,
        compiler_params=pltpu.CompilerParams(vmem_limit_bytes=48 * 2**20),
        name="spread_weights",
    )(legend)


def spectra_kernel(bands, first_group, pairs, weights, *refs):
    held = refs[:bands]
    out, block, sems = refs[-3:]
    width = held[0].shape[1]
    tall = held[0].shape[0]
    groups = pl.cdiv(pairs, GROUP)
    part = tall // groups
    member = lax.broadcasted_iota(jnp.int32, (2 * GROUP, width), 0) % GROUP
    masks = [jnp.tile((member == i).astype(F32).astype(BF16), (bands * part // (2 * GROUP), 1)) for i in range(GROUP)]
    copies = []
    for g in range(groups):
        stacked = jnp.concatenate([ref[g * part:(g + 1) * part, :] for ref in held], axis=0)
        for at in range(0, min(GROUP, pairs - g * GROUP), 2):
            both = jnp.concatenate([stacked * masks[at], stacked * masks[at + 1]], axis=1)
            product = jnp.dot(weights[first_group + g], both, preferred_element_type=F32)
            pair = g * GROUP + at
            block[pair] = product[:, :width]
            block[pair + 1] = product[:, width:]
            copy = pltpu.make_async_copy(
                block.at[pl.ds(pair, 2)], out.at[pl.ds(first_group * GROUP + pair, 2)], sems.at[pair // 2]
            )
            copy.start()
            copies.append(copy)
    for copy in copies:
        copy.wait()


def spectra_part(weights, held, out, pair_count, first_group, groups):
    bands = len(held)
    width = held[0].shape[1]
    slots = weights.shape[1]
    pairs = min(groups * GROUP, pair_count - first_group * GROUP)
    previous = [] if out is None else [out]
    vmem = pl.BlockSpec(memory_space=pltpu.VMEM)
    anywhere = pl.BlockSpec(memory_space=pl.ANY)
    return pl.pallas_call(
        functools.partial(spectra_kernel, bands, first_group, pairs),
        out_shape=jax.ShapeDtypeStruct((pair_count, slots, width), F32),
        in_specs=[vmem] * (1 + bands) + [anywhere] * len(previous),
        out_specs=anywhere,
        input_output_aliases={1 + bands: 0} if previous else {},
        scratch_shapes=[pltpu.VMEM((pairs, slots, width), F32), pltpu.SemaphoreType.DMA((pairs // 2,))],
        compiler_params=pltpu.CompilerParams(vmem_limit_bytes=48 * 2**20),
        name="spectra_part",
    )(weights, *held, *previous)


def swap(axis, size, step):
    return [(i, i ^ step) for i in range(size)]


def exchange(array, axis, steps):
    return [lax.ppermute(part, axis, swap(axis, lax.axis_size(axis), step)) for part, step in zip(array, steps)]


def shards(grid, row_points, legendre):
    set_size = lax.axis_size("set")
    band_size = lax.axis_size("band")
    rows, points, width = grid.shape
    pair_count = legendre.shape[0]
    slots = legendre.shape[2] // band_size
    peers = set_size // 2
    flat = grid.transpose(1, 0, 2).reshape(points * rows, width)
    theirs = lax.ppermute(flat, "set", swap("set", set_size, 1))
    mine, factor = prepare(row_points, flat, peers, pair_count)
    legend = lax.dynamic_slice_in_dim(legendre, lax.axis_index("band") * slots, slots, 2)
    weights = spread_weights(legend, rows, band_size)
    all_groups = pl.cdiv(pair_count, GROUP)
    cut = (all_groups + 1) // 2
    out = None
    steps = list(range(1, peers, 2)) + list(range(2, peers, 2))[::-1]
    chunks = ((0, cut), (cut, all_groups - cut))
    gathered = []
    partial = []
    for first_group, groups in chunks:
        parts = list(fourier_sums(row_points, mine, theirs, factor, groups, first_group, peers, pair_count))
        if not partial:
            theirs = parts.pop()
        partial.append(parts)
    for parts in partial:
        arrived = exchange([parts[k].astype(WIRE) for k in steps], "set", [2 * k for k in steps])
        if gathered:
            arrived, weights, gathered[0] = lax.optimization_barrier((arrived, weights, gathered[0]))
        total = parts[0]
        for part in arrived:
            total = total + part.astype(F32)
        rounded = total.astype(BF16)
        turns = list(range(1, band_size))
        gathered.append([rounded] + exchange([rounded] * len(turns), "band", turns))
    for held, (first_group, groups) in zip(gathered, chunks):
        out = spectra_part(weights, held, out, pair_count, first_group, groups)
    return out


def solution(mesh):
    return jax.shard_map(
        shards,
        mesh=mesh,
        in_specs=(P("band", "set", None), P("band"), P("set", None, None)),
        out_specs=P("set", "band", None),
        check_vma=False,
    )
```

```python
import functools
import math

import jax
import jax.numpy as jnp
from jax import lax
from jax.experimental import pallas as pl
from jax.experimental.pallas import tpu as pltpu
from jax.sharding import PartitionSpec as P

TRUNC = 1279
GROUP = 8
F32 = jnp.float32
BF16 = jnp.bfloat16
WIRE = jnp.float16
VMEM = 16 * 2**20


def round_up(value, step):
    return -(-value // step) * step


def unit_circle(multiplier, point, length, inverse):
    product = (multiplier * point).astype(F32)
    residue = product - jnp.floor(product * inverse + 0.5) * length
    quarters = 4.0 * residue * inverse
    turn = jnp.floor(quarters + 0.5)
    angle = (quarters - turn) * (0.5 * math.pi)
    square = angle * angle
    sine = angle * (1.0 + square * (-1 / 6 + square * (1 / 120 + square * (-1 / 5040 + square / 362880))))
    cosine = 1.0 + square * (-0.5 + square * (1 / 24 + square * (-1 / 720 + square / 40320)))
    quadrant = turn.astype(jnp.int32) & 3
    odd = (quadrant & 1) == 1
    real = jnp.where(odd, sine, cosine)
    imag = jnp.where(odd, cosine, sine)
    real = jnp.where((quadrant == 1) | (quadrant == 2), -real, real)
    imag = jnp.where(quadrant >= 2, imag, -imag)
    return real, imag


def rotate(a, b):
    return a[0] * b[0] - a[1] * b[1], a[0] * b[1] + a[1] * b[0]


def split(values):
    high = values.astype(BF16)
    return high, (values - high.astype(F32)).astype(BF16)


def prepare_values(raw, start, length, length_int):
    width = raw.shape[1]
    lane = lax.broadcasted_iota(jnp.int32, (1, width), 1)
    where = start + lax.broadcasted_iota(jnp.int32, (raw.shape[0], 1), 0)
    folded = pltpu.roll(raw, width // 2, 1) + jnp.where(lane < width // 2, raw, -raw)
    scale = lax.rsqrt(jnp.full((1, width), length, F32))
    return split(jnp.where(where < length_int, folded * scale, 0.0))


def store_values(out, r, side, raw, start, length_int):
    points, width = raw.shape
    depth = out.shape[1] // 3
    lanes = slice(side * width, (side + 1) * width)
    high, low = prepare_values(raw, start, length_int.astype(F32), length_int)
    for part, values in enumerate((high, low, high)):
        out[r, part * depth:part * depth + points, lanes] = values
        rest = jnp.zeros((depth - points, width), BF16)
        out[r, part * depth + points:(part + 1) * depth, lanes] = rest


def row_of(block, r, rows):
    return block[pl.ds(r, block.shape[0] // rows, stride=rows), :]


def prepare_kernel(peers, pair_count, points, row_points, factor):
    rows, _, tall, depth = factor.shape
    held = round_up(pl.cdiv(pair_count, GROUP), GROUP)
    set_index = lax.axis_index("set")
    start = set_index * points
    beside = (set_index ^ 1) * points - start
    slot = lax.broadcasted_iota(jnp.int32, (1, depth), 1)
    point = jnp.where(slot < round_up(points, 128), start + slot, beside)
    heads = round_up(peers + 1, GROUP)
    sub = lax.broadcasted_iota(jnp.int32, (GROUP + heads + held, 1), 0)
    order = sub - GROUP
    head = jnp.where(order < peers, (set_index ^ (2 * order)) * pair_count, TRUNC)
    multiplier = jnp.where(sub < GROUP, sub, jnp.where(order < heads, head, (order - heads) * GROUP))
    for r in range(rows):
        length = row_points[r].astype(F32)
        real, imag = unit_circle(multiplier, point, length, 1.0 / length)
        factor[r, 0, :GROUP, :] = real[:GROUP]
        factor[r, 1, :GROUP, :] = imag[:GROUP]
        last = GROUP + peers
        factor[r, 0, GROUP:2 * GROUP, :] = jnp.broadcast_to(real[last:last + 1], (GROUP, depth))
        factor[r, 1, GROUP:2 * GROUP, :] = jnp.broadcast_to(imag[last:last + 1], (GROUP, depth))
        tail = real[GROUP + heads:], imag[GROUP + heads:]
        for peer in range(peers):
            at = GROUP + peer
            base = rotate((real[at:at + 1], imag[at:at + 1]), tail)
            to = 2 * GROUP + peer * held
            factor[r, 0, to:to + held, :] = base[0]
            factor[r, 1, to:to + held, :] = base[1]


def prepare(row_points, points, peers, pair_count):
    rows = row_points.shape[0]
    tall = 2 * GROUP + peers * round_up(pl.cdiv(pair_count, GROUP), GROUP)
    return pl.pallas_call(
        functools.partial(prepare_kernel, peers, pair_count, points),
        out_shape=jax.ShapeDtypeStruct((rows, 2, tall, round_up(points, 128) + 128), F32),
        in_specs=[pl.BlockSpec(memory_space=pltpu.SMEM)],
        out_specs=pl.BlockSpec(memory_space=pltpu.VMEM),
        compiler_params=pltpu.CompilerParams(vmem_limit_bytes=VMEM),
        cost_estimate=pl.CostEstimate(flops=1 << 22, bytes_accessed=1 << 22, transcendentals=0),
        name="prepare",
    )(row_points)


def fourier_kernel(groups, first_group, peers, pair_count, fresh, row_points, factor, *refs):
    table, sums, twist = refs[-3:]
    blocks, outs = refs[:1 + fresh], refs[1 + fresh:1 + fresh + peers]
    rows = table.shape[0]
    width = outs[0].shape[1]
    depth = table.shape[2] // 3
    held = round_up(pl.cdiv(pair_count, GROUP), GROUP)
    set_index = lax.axis_index("set")
    values = refs[1 + fresh + peers] if fresh else blocks[0]
    if fresh:
        points = blocks[0].shape[0] // rows
        for side, block in enumerate(blocks):
            for r in range(rows):
                store_values(values, r, side, row_of(block, r, rows), (set_index ^ side) * points, row_points[r])
    lane = lax.broadcasted_iota(jnp.int32, (1, width), 1)
    north = lane < width // 2
    sub = lax.broadcasted_iota(jnp.int32, (GROUP, 1), 0)
    for r in range(rows):
        near = factor[r, 0, :GROUP, :], factor[r, 1, :GROUP, :]
        last = factor[r, 0, GROUP:2 * GROUP, :], factor[r, 1, GROUP:2 * GROUP, :]
        for index in range(peers * groups):
            at = 2 * GROUP + index // groups * held + first_group + index % groups
            base = factor[r, 0, at:at + 1, :], factor[r, 1, at:at + 1, :]
            first = rotate(base, near)
            second = rotate(last, (first[0], -first[1]))
            block = jnp.concatenate([*first, *second], axis=0)
            high, low = split(block[:, :depth])
            lines = slice(index * 4 * GROUP, (index + 1) * 4 * GROUP)
            for part, piece in enumerate((high, high, low)):
                table[r, lines, part * depth:(part + 1) * depth] = piece
            twist[r, lines, :] = block[:, depth:]
        sums[r] = jnp.dot(table[r], values[r], preferred_element_type=F32)
    for peer in range(peers):
        for g in range(groups):
            base = (set_index ^ (2 * peer)) * pair_count + (first_group + g) * GROUP
            for side in range(2):
                wave = base + sub
                wave = TRUNC - wave if side else wave
                at = ((peer * groups + g) * 2 + side) * 2 * GROUP
                for r in range(rows):
                    turn = twist[r, at:at + GROUP, :], twist[r, at + GROUP:at + 2 * GROUP, :]
                    far = sums[r, at:at + GROUP, width:], sums[r, at + GROUP:at + 2 * GROUP, width:]
                    far = rotate(turn, far)
                    real = sums[r, at:at + GROUP, :width] + far[0]
                    imag = sums[r, at + GROUP:at + 2 * GROUP, :width] + far[1]
                    usable = wave <= (row_points[r] - 1) // 2
                    even = jnp.where(north, real, pltpu.roll(imag, width // 2, 1))
                    odd = jnp.where(north, pltpu.roll(real, width // 2, 1), imag)
                    for parity, block in enumerate((even, odd)):
                        to = (((g * 2 + side) * 2 + parity) * rows + r) * GROUP
                        outs[peer][to:to + GROUP, :] = jnp.where(usable, block, 0.0)


def fourier_sums(row_points, factor, blocks, groups, first_group, peers, pair_count):
    rows = row_points.shape[0]
    depth = factor.shape[3] - 128
    fresh = len(blocks) > 1
    width = blocks[0].shape[-1] // (1 if fresh else 2)
    out_rows = groups * 4 * rows * GROUP
    tall = peers * groups * 4 * GROUP
    vmem = pl.BlockSpec(memory_space=pltpu.VMEM)
    out_shape = [jax.ShapeDtypeStruct((out_rows, width), F32)] * peers
    out_shape += [jax.ShapeDtypeStruct((rows, 3 * depth, 2 * width), BF16)] if fresh else []
    return pl.pallas_call(
        functools.partial(fourier_kernel, groups, first_group, peers, pair_count, fresh),
        out_shape=out_shape,
        in_specs=[pl.BlockSpec(memory_space=pltpu.SMEM), vmem] + [vmem] * len(blocks),
        out_specs=[vmem] * len(out_shape),
        scratch_shapes=[
            pltpu.VMEM((rows, tall, 3 * depth), BF16),
            pltpu.VMEM((rows, tall, 2 * width), F32),
            pltpu.VMEM((rows, tall, 128), F32),
        ],
        compiler_params=pltpu.CompilerParams(vmem_limit_bytes=VMEM),
        name="fourier_sums",
    )(row_points, factor, *blocks)


def weights_kernel(rows, bands, legend, out):
    pair_count, total, slots = legend.shape
    wide = out.shape[2]
    band_index = lax.axis_index("band")
    first_pair = lax.axis_index("set") * pair_count
    source = lax.broadcasted_iota(jnp.int32, (GROUP * total, 1), 0)
    lane = lax.broadcasted_iota(jnp.int32, (1, wide), 1)
    member = lane % GROUP
    row = lane // GROUP % rows
    parity = lane // (GROUP * rows) % 2
    side = lane // (GROUP * rows * 2) % 2
    band = (lane // (GROUP * rows * 4)) ^ band_index
    spread = (source == member * total + band * rows + row).astype(F32).astype(BF16)
    slot = band_index * slots + lax.broadcasted_iota(jnp.int32, (slots, 1), 0)
    for group in range(out.shape[0]):
        count = min(GROUP, pair_count - group * GROUP)
        held = legend[group * GROUP:group * GROUP + count].astype(F32).reshape(count * total, slots)
        if count < GROUP:
            held = jnp.concatenate([held, jnp.zeros(((GROUP - count) * total, slots), F32)], axis=0)
        moved = lax.dot_general(
            held.astype(BF16), spread, (((0,), (0,)), ((), ())), preferred_element_type=F32
        )
        first = TRUNC - (first_pair + group * GROUP + member)
        start = jnp.where(side == 0, 0, first + 1)
        sign = 1 - 2 * side
        match = (((slot - start) & 1) == parity) & (sign * slot <= sign * first - side)
        out[group] = jnp.where(match, moved, 0.0).astype(BF16)


def spread_weights(legend, rows, bands):
    pair_count, total, slots = legend.shape
    groups = pl.cdiv(pair_count, GROUP)
    vmem = pl.BlockSpec(memory_space=pltpu.VMEM)
    return pl.pallas_call(
        functools.partial(weights_kernel, rows, bands),
        out_shape=jax.ShapeDtypeStruct((groups, slots, bands * 4 * rows * GROUP), BF16),
        in_specs=[vmem],
        out_specs=vmem,
        compiler_params=pltpu.CompilerParams(vmem_limit_bytes=VMEM),
        name="spread_weights",
    )(legend)


def spectra_kernel(bands, first_group, pairs, weights, *refs):
    held = refs[:bands]
    out, block, sems = refs[-3:]
    width = held[0].shape[1]
    tall = held[0].shape[0]
    groups = pl.cdiv(pairs, GROUP)
    part = tall // groups
    member = lax.broadcasted_iota(jnp.int32, (2 * GROUP, width), 0) % GROUP
    masks = [jnp.tile((member == i).astype(F32).astype(BF16), (bands * part // (2 * GROUP), 1)) for i in range(GROUP)]
    copies = []
    for g in range(groups):
        stacked = jnp.concatenate([ref[g * part:(g + 1) * part, :] for ref in held], axis=0)
        for at in range(0, min(GROUP, pairs - g * GROUP), 2):
            both = jnp.concatenate([stacked * masks[at], stacked * masks[at + 1]], axis=1)
            product = jnp.dot(weights[first_group + g], both, preferred_element_type=F32)
            pair = g * GROUP + at
            block[pair] = product[:, :width]
            block[pair + 1] = product[:, width:]
            copy = pltpu.make_async_copy(
                block.at[pl.ds(pair, 2)], out.at[pl.ds(first_group * GROUP + pair, 2)], sems.at[pair // 2]
            )
            copy.start()
            copies.append(copy)
    for copy in copies:
        copy.wait()


def spectra_part(weights, held, out, pair_count, first_group, groups):
    bands = len(held)
    width = held[0].shape[1]
    slots = weights.shape[1]
    pairs = min(groups * GROUP, pair_count - first_group * GROUP)
    previous = [] if out is None else [out]
    vmem = pl.BlockSpec(memory_space=pltpu.VMEM)
    anywhere = pl.BlockSpec(memory_space=pl.ANY)
    return pl.pallas_call(
        functools.partial(spectra_kernel, bands, first_group, pairs),
        out_shape=jax.ShapeDtypeStruct((pair_count, slots, width), F32),
        in_specs=[vmem] * (1 + bands) + [anywhere] * len(previous),
        out_specs=anywhere,
        input_output_aliases={1 + bands: 0} if previous else {},
        scratch_shapes=[pltpu.VMEM((pairs, slots, width), F32), pltpu.SemaphoreType.DMA((pairs // 2,))],
        compiler_params=pltpu.CompilerParams(vmem_limit_bytes=VMEM),
        name="spectra_part",
    )(weights, *held, *previous)


def swap(axis, size, step):
    return [(i, i ^ step) for i in range(size)]


def exchange(array, axis, steps):
    return [lax.ppermute(part, axis, swap(axis, lax.axis_size(axis), step)) for part, step in zip(array, steps)]


def shards(grid, row_points, legendre):
    set_size = lax.axis_size("set")
    band_size = lax.axis_size("band")
    rows, points, width = grid.shape
    pair_count = legendre.shape[0]
    slots = legendre.shape[2] // band_size
    peers = set_size // 2
    flat = grid.transpose(1, 0, 2).reshape(points * rows, width)
    theirs = lax.ppermute(flat, "set", swap("set", set_size, 1))
    factor = prepare(row_points, points, peers, pair_count)
    blocks = [flat, theirs]
    legend = lax.dynamic_slice_in_dim(legendre, lax.axis_index("band") * slots, slots, 2)
    weights = spread_weights(legend, rows, band_size)
    all_groups = pl.cdiv(pair_count, GROUP)
    cut = (all_groups + 1) // 2
    out = None
    steps = list(range(1, peers, 2)) + list(range(2, peers, 2))[::-1]
    chunks = ((0, cut), (cut, all_groups - cut))
    gathered = []
    partial = []
    for first_group, groups in chunks:
        parts = list(fourier_sums(row_points, factor, blocks, groups, first_group, peers, pair_count))
        if not partial:
            blocks = [parts.pop()]
        partial.append(parts)
    for parts in partial:
        arrived = exchange([parts[k].astype(WIRE) for k in steps], "set", [2 * k for k in steps])
        if gathered:
            arrived, weights, gathered[0] = lax.optimization_barrier((arrived, weights, gathered[0]))
        total = parts[0]
        for part in arrived:
            total = total + part.astype(F32)
        rounded = total.astype(BF16)
        turns = list(range(1, band_size))
        gathered.append([rounded] + exchange([rounded] * len(turns), "band", turns))
    for held, (first_group, groups) in zip(gathered, chunks):
        out = spectra_part(weights, held, out, pair_count, first_group, groups)
    return out


def solution(mesh):
    return jax.shard_map(
        shards,
        mesh=mesh,
        in_specs=(P("band", "set", None), P("band"), P("set", None, None)),
        out_specs=P("set", "band", None),
        check_vma=False,
    )
```

```python
import functools
import math

import jax
import jax.numpy as jnp
from jax import lax
from jax.experimental import pallas as pl
from jax.experimental.pallas import tpu as pltpu
from jax.sharding import PartitionSpec as P

TRUNC = 1279
GROUP = 8
F32 = jnp.float32
BF16 = jnp.bfloat16
WIRE = jnp.float16
VMEM = 16 * 2**20


def round_up(value, step):
    return -(-value // step) * step


def unit_circle(multiplier, point, length, inverse):
    product = (multiplier * point).astype(F32)
    residue = product - jnp.floor(product * inverse + 0.5) * length
    quarters = 4.0 * residue * inverse
    turn = jnp.floor(quarters + 0.5)
    angle = (quarters - turn) * (0.5 * math.pi)
    square = angle * angle
    sine = angle * (1.0 + square * (-1 / 6 + square * (1 / 120 + square * (-1 / 5040 + square / 362880))))
    cosine = 1.0 + square * (-0.5 + square * (1 / 24 + square * (-1 / 720 + square / 40320)))
    quadrant = turn.astype(jnp.int32) & 3
    odd = (quadrant & 1) == 1
    real = jnp.where(odd, sine, cosine)
    imag = jnp.where(odd, cosine, sine)
    real = jnp.where((quadrant == 1) | (quadrant == 2), -real, real)
    imag = jnp.where(quadrant >= 2, imag, -imag)
    return real, imag


def rotate(a, b):
    return a[0] * b[0] - a[1] * b[1], a[0] * b[1] + a[1] * b[0]


def split(values):
    high = values.astype(BF16)
    return high, (values - high.astype(F32)).astype(BF16)


def prepare_values(raw, start, length, length_int):
    width = raw.shape[1]
    lane = lax.broadcasted_iota(jnp.int32, (1, width), 1)
    where = start + lax.broadcasted_iota(jnp.int32, (raw.shape[0], 1), 0)
    folded = pltpu.roll(raw, width // 2, 1) + jnp.where(lane < width // 2, raw, -raw)
    scale = lax.rsqrt(jnp.full((1, width), length, F32))
    return split(jnp.where(where < length_int, folded * scale, 0.0))


def store_values(out, r, side, raw, start, length_int):
    points, width = raw.shape
    depth = out.shape[1] // 3
    lanes = slice(side * width, (side + 1) * width)
    high, low = prepare_values(raw, start, length_int.astype(F32), length_int)
    for part, values in enumerate((high, low, high)):
        out[r, part * depth:part * depth + points, lanes] = values
        rest = jnp.zeros((depth - points, width), BF16)
        out[r, part * depth + points:(part + 1) * depth, lanes] = rest


def row_of(block, r, rows):
    return block[pl.ds(r, block.shape[0] // rows, stride=rows), :]


def prepare_kernel(peers, pair_count, points, row_points, factor):
    rows, _, tall, depth = factor.shape
    held = round_up(pl.cdiv(pair_count, GROUP), GROUP)
    set_index = lax.axis_index("set")
    start = set_index * points
    beside = (set_index ^ 1) * points - start
    slot = lax.broadcasted_iota(jnp.int32, (1, depth), 1)
    point = jnp.where(slot < round_up(points, 128), start + slot, beside)
    heads = round_up(peers + 1, GROUP)
    sub = lax.broadcasted_iota(jnp.int32, (GROUP + heads + held, 1), 0)
    order = sub - GROUP
    head = jnp.where(order < peers, (set_index ^ (2 * order)) * pair_count, TRUNC)
    multiplier = jnp.where(sub < GROUP, sub, jnp.where(order < heads, head, (order - heads) * GROUP))
    for r in range(rows):
        length = row_points[r].astype(F32)
        real, imag = unit_circle(multiplier, point, length, 1.0 / length)
        factor[r, 0, :GROUP, :] = real[:GROUP]
        factor[r, 1, :GROUP, :] = imag[:GROUP]
        last = GROUP + peers
        factor[r, 0, GROUP:2 * GROUP, :] = jnp.broadcast_to(real[last:last + 1], (GROUP, depth))
        factor[r, 1, GROUP:2 * GROUP, :] = jnp.broadcast_to(imag[last:last + 1], (GROUP, depth))
        tail = real[GROUP + heads:], imag[GROUP + heads:]
        for peer in range(peers):
            at = GROUP + peer
            base = rotate((real[at:at + 1], imag[at:at + 1]), tail)
            to = 2 * GROUP + peer * held
            factor[r, 0, to:to + held, :] = base[0]
            factor[r, 1, to:to + held, :] = base[1]


def prepare(row_points, points, peers, pair_count):
    rows = row_points.shape[0]
    tall = 2 * GROUP + peers * round_up(pl.cdiv(pair_count, GROUP), GROUP)
    return pl.pallas_call(
        functools.partial(prepare_kernel, peers, pair_count, points),
        out_shape=jax.ShapeDtypeStruct((rows, 2, tall, round_up(points, 128) + 128), F32),
        in_specs=[pl.BlockSpec(memory_space=pltpu.SMEM)],
        out_specs=pl.BlockSpec(memory_space=pltpu.VMEM),
        compiler_params=pltpu.CompilerParams(vmem_limit_bytes=VMEM),
        cost_estimate=pl.CostEstimate(flops=1 << 22, bytes_accessed=1 << 22, transcendentals=0),
        name="prepare",
    )(row_points)


def fourier_kernel(groups, first_group, peers, pair_count, row_points, factor, mine, theirs, *refs):
    outs = refs[:peers]
    values, table, sums, twist = refs[peers:]
    rows = table.shape[0]
    width = outs[0].shape[1]
    depth = table.shape[2] // 3
    held = round_up(pl.cdiv(pair_count, GROUP), GROUP)
    set_index = lax.axis_index("set")
    points = mine.shape[0] // rows
    for side, block in enumerate((mine, theirs)):
        for r in range(rows):
            store_values(values, r, side, row_of(block, r, rows), (set_index ^ side) * points, row_points[r])
    lane = lax.broadcasted_iota(jnp.int32, (1, width), 1)
    north = lane < width // 2
    sub = lax.broadcasted_iota(jnp.int32, (GROUP, 1), 0)
    for r in range(rows):
        near = factor[r, 0, :GROUP, :], factor[r, 1, :GROUP, :]
        last = factor[r, 0, GROUP:2 * GROUP, :], factor[r, 1, GROUP:2 * GROUP, :]
        for index in range(peers * groups):
            at = 2 * GROUP + index // groups * held + first_group + index % groups
            base = factor[r, 0, at:at + 1, :], factor[r, 1, at:at + 1, :]
            first = rotate(base, near)
            second = rotate(last, (first[0], -first[1]))
            block = jnp.concatenate([*first, *second], axis=0)
            high, low = split(block[:, :depth])
            lines = slice(index * 4 * GROUP, (index + 1) * 4 * GROUP)
            for part, piece in enumerate((high, high, low)):
                table[r, lines, part * depth:(part + 1) * depth] = piece
            twist[r, lines, :] = block[:, depth:]
        sums[r] = jnp.dot(table[r], values[r], preferred_element_type=F32)
    for peer in range(peers):
        for g in range(groups):
            base = (set_index ^ (2 * peer)) * pair_count + (first_group + g) * GROUP
            for side in range(2):
                wave = base + sub
                wave = TRUNC - wave if side else wave
                at = ((peer * groups + g) * 2 + side) * 2 * GROUP
                for r in range(rows):
                    turn = twist[r, at:at + GROUP, :], twist[r, at + GROUP:at + 2 * GROUP, :]
                    far = sums[r, at:at + GROUP, width:], sums[r, at + GROUP:at + 2 * GROUP, width:]
                    far = rotate(turn, far)
                    real = sums[r, at:at + GROUP, :width] + far[0]
                    imag = sums[r, at + GROUP:at + 2 * GROUP, :width] + far[1]
                    usable = wave <= (row_points[r] - 1) // 2
                    even = jnp.where(north, real, pltpu.roll(imag, width // 2, 1))
                    odd = jnp.where(north, pltpu.roll(real, width // 2, 1), imag)
                    for parity, block in enumerate((even, odd)):
                        to = (((g * 2 + side) * 2 + parity) * rows + r) * GROUP
                        outs[peer][to:to + GROUP, :] = jnp.where(usable, block, 0.0)


def fourier_sums(row_points, factor, mine, theirs, groups, first_group, peers, pair_count):
    rows = row_points.shape[0]
    depth = factor.shape[3] - 128
    width = mine.shape[1]
    out_rows = groups * 4 * rows * GROUP
    tall = peers * groups * 4 * GROUP
    vmem = pl.BlockSpec(memory_space=pltpu.VMEM)
    return pl.pallas_call(
        functools.partial(fourier_kernel, groups, first_group, peers, pair_count),
        out_shape=[jax.ShapeDtypeStruct((out_rows, width), F32)] * peers,
        in_specs=[pl.BlockSpec(memory_space=pltpu.SMEM)] + [vmem] * 3,
        out_specs=[vmem] * peers,
        scratch_shapes=[
            pltpu.VMEM((rows, 3 * depth, 2 * width), BF16),
            pltpu.VMEM((rows, tall, 3 * depth), BF16),
            pltpu.VMEM((rows, tall, 2 * width), F32),
            pltpu.VMEM((rows, tall, 128), F32),
        ],
        compiler_params=pltpu.CompilerParams(vmem_limit_bytes=VMEM),
        name="fourier_sums",
    )(row_points, factor, mine, theirs)


def weights_kernel(rows, bands, legend, out):
    pair_count, total, slots = legend.shape
    wide = out.shape[2]
    band_index = lax.axis_index("band")
    first_pair = lax.axis_index("set") * pair_count
    source = lax.broadcasted_iota(jnp.int32, (GROUP * total, 1), 0)
    lane = lax.broadcasted_iota(jnp.int32, (1, wide), 1)
    member = lane % GROUP
    row = lane // GROUP % rows
    parity = lane // (GROUP * rows) % 2
    side = lane // (GROUP * rows * 2) % 2
    band = (lane // (GROUP * rows * 4)) ^ band_index
    spread = (source == member * total + band * rows + row).astype(F32).astype(BF16)
    slot = band_index * slots + lax.broadcasted_iota(jnp.int32, (slots, 1), 0)
    for group in range(out.shape[0]):
        count = min(GROUP, pair_count - group * GROUP)
        held = legend[group * GROUP:group * GROUP + count].astype(F32).reshape(count * total, slots)
        if count < GROUP:
            held = jnp.concatenate([held, jnp.zeros(((GROUP - count) * total, slots), F32)], axis=0)
        moved = lax.dot_general(
            held.astype(BF16), spread, (((0,), (0,)), ((), ())), preferred_element_type=F32
        )
        first = TRUNC - (first_pair + group * GROUP + member)
        start = jnp.where(side == 0, 0, first + 1)
        sign = 1 - 2 * side
        match = (((slot - start) & 1) == parity) & (sign * slot <= sign * first - side)
        out[group] = jnp.where(match, moved, 0.0).astype(BF16)


def spread_weights(legend, rows, bands):
    pair_count, total, slots = legend.shape
    groups = pl.cdiv(pair_count, GROUP)
    vmem = pl.BlockSpec(memory_space=pltpu.VMEM)
    return pl.pallas_call(
        functools.partial(weights_kernel, rows, bands),
        out_shape=jax.ShapeDtypeStruct((groups, slots, bands * 4 * rows * GROUP), BF16),
        in_specs=[vmem],
        out_specs=vmem,
        compiler_params=pltpu.CompilerParams(vmem_limit_bytes=VMEM),
        name="spread_weights",
    )(legend)


def spectra_kernel(bands, first_group, pairs, weights, *refs):
    held = refs[:bands]
    out, block, sems = refs[-3:]
    width = held[0].shape[1]
    tall = held[0].shape[0]
    groups = pl.cdiv(pairs, GROUP)
    part = tall // groups
    member = lax.broadcasted_iota(jnp.int32, (2 * GROUP, width), 0) % GROUP
    masks = [jnp.tile((member == i).astype(F32).astype(BF16), (bands * part // (2 * GROUP), 1)) for i in range(GROUP)]
    copies = []
    for g in range(groups):
        stacked = jnp.concatenate([ref[g * part:(g + 1) * part, :] for ref in held], axis=0)
        for at in range(0, min(GROUP, pairs - g * GROUP), 2):
            both = jnp.concatenate([stacked * masks[at], stacked * masks[at + 1]], axis=1)
            product = jnp.dot(weights[first_group + g], both, preferred_element_type=F32)
            pair = g * GROUP + at
            block[pair] = product[:, :width]
            block[pair + 1] = product[:, width:]
            copy = pltpu.make_async_copy(
                block.at[pl.ds(pair, 2)], out.at[pl.ds(first_group * GROUP + pair, 2)], sems.at[pair // 2]
            )
            copy.start()
            copies.append(copy)
    for copy in copies:
        copy.wait()


def spectra_part(weights, held, out, pair_count, first_group, groups):
    bands = len(held)
    width = held[0].shape[1]
    slots = weights.shape[1]
    pairs = min(groups * GROUP, pair_count - first_group * GROUP)
    previous = [] if out is None else [out]
    vmem = pl.BlockSpec(memory_space=pltpu.VMEM)
    anywhere = pl.BlockSpec(memory_space=pl.ANY)
    return pl.pallas_call(
        functools.partial(spectra_kernel, bands, first_group, pairs),
        out_shape=jax.ShapeDtypeStruct((pair_count, slots, width), F32),
        in_specs=[vmem] * (1 + bands) + [anywhere] * len(previous),
        out_specs=anywhere,
        input_output_aliases={1 + bands: 0} if previous else {},
        scratch_shapes=[pltpu.VMEM((pairs, slots, width), F32), pltpu.SemaphoreType.DMA((pairs // 2,))],
        compiler_params=pltpu.CompilerParams(vmem_limit_bytes=VMEM),
        name="spectra_part",
    )(weights, *held, *previous)


def swap(axis, size, step):
    return [(i, i ^ step) for i in range(size)]


def exchange(array, axis, steps):
    return [lax.ppermute(part, axis, swap(axis, lax.axis_size(axis), step)) for part, step in zip(array, steps)]


def shards(grid, row_points, legendre):
    set_size = lax.axis_size("set")
    band_size = lax.axis_size("band")
    rows, points, width = grid.shape
    pair_count = legendre.shape[0]
    slots = legendre.shape[2] // band_size
    peers = set_size // 2
    flat = grid.transpose(1, 0, 2).reshape(points * rows, width)
    theirs = lax.ppermute(flat, "set", swap("set", set_size, 1))
    factor = prepare(row_points, points, peers, pair_count)
    legend = lax.dynamic_slice_in_dim(legendre, lax.axis_index("band") * slots, slots, 2)
    weights = spread_weights(legend, rows, band_size)
    all_groups = pl.cdiv(pair_count, GROUP)
    cut = (all_groups + 1) // 2
    chunks = ((0, cut), (cut, all_groups - cut))
    gathered = []
    partial = []
    for first_group, groups in chunks:
        partial.append(fourier_sums(row_points, factor, flat, theirs, groups, first_group, peers, pair_count))
    for parts in partial:
        steps = list(range(1, peers))
        steps = steps[::-1] if gathered else steps[::2] + steps[1::2]
        arrived = exchange([parts[k].astype(WIRE) for k in steps], "set", [2 * k for k in steps])
        if gathered:
            arrived, weights, gathered[0] = lax.optimization_barrier((arrived, weights, gathered[0]))
        total = parts[0]
        for part in arrived:
            total = total + part.astype(F32)
        rounded = total.astype(BF16)
        turns = list(range(1, band_size))
        gathered.append([rounded] + exchange([rounded] * len(turns), "band", turns))
    out = None
    for held, (first_group, groups) in zip(gathered, chunks):
        out = spectra_part(weights, held, out, pair_count, first_group, groups)
    return out


def solution(mesh):
    return jax.shard_map(
        shards,
        mesh=mesh,
        in_specs=(P("band", "set", None), P("band"), P("set", None, None)),
        out_specs=P("set", "band", None),
        check_vma=False,
    )
```

```python
import functools
import math

import jax
import jax.numpy as jnp
from jax import lax
from jax.experimental import pallas as pl
from jax.experimental.pallas import tpu as pltpu
from jax.sharding import PartitionSpec as P

TRUNC = 1279
GROUP = 8
F32 = jnp.float32
BF16 = jnp.bfloat16
WIRE = jnp.float16
VMEM = 16 * 2**20


def round_up(value, step):
    return -(-value // step) * step


def unit_circle(multiplier, point, length, inverse):
    product = (multiplier * point).astype(F32)
    residue = product - jnp.floor(product * inverse + 0.5) * length
    quarters = 4.0 * residue * inverse
    turn = jnp.floor(quarters + 0.5)
    angle = (quarters - turn) * (0.5 * math.pi)
    square = angle * angle
    sine = angle * (1.0 + square * (-1 / 6 + square * (1 / 120 + square * (-1 / 5040 + square / 362880))))
    cosine = 1.0 + square * (-0.5 + square * (1 / 24 + square * (-1 / 720 + square / 40320)))
    quadrant = turn.astype(jnp.int32) & 3
    odd = (quadrant & 1) == 1
    real = jnp.where(odd, sine, cosine)
    imag = jnp.where(odd, cosine, sine)
    real = jnp.where((quadrant == 1) | (quadrant == 2), -real, real)
    imag = jnp.where(quadrant >= 2, imag, -imag)
    return real, imag


def micros(count):
    return pl.CostEstimate(flops=0, bytes_accessed=count * 3 * 10**6, transcendentals=0)


def rotate(a, b):
    return a[0] * b[0] - a[1] * b[1], a[0] * b[1] + a[1] * b[0]


def split(values):
    high = values.astype(BF16)
    return high, (values - high.astype(F32)).astype(BF16)


def prepare_values(raw, start, length, length_int):
    width = raw.shape[1]
    lane = lax.broadcasted_iota(jnp.int32, (1, width), 1)
    where = start + lax.broadcasted_iota(jnp.int32, (raw.shape[0], 1), 0)
    folded = pltpu.roll(raw, width // 2, 1) + jnp.where(lane < width // 2, raw, -raw)
    scale = lax.rsqrt(jnp.full((1, width), length, F32))
    return split(jnp.where(where < length_int, folded * scale, 0.0))


def store_values(out, r, side, raw, start, length_int):
    points, width = raw.shape
    depth = out.shape[1] // 3
    lanes = slice(side * width, (side + 1) * width)
    high, low = prepare_values(raw, start, length_int.astype(F32), length_int)
    for part, values in enumerate((high, low, high)):
        out[r, part * depth:part * depth + points, lanes] = values
        rest = jnp.zeros((depth - points, width), BF16)
        out[r, part * depth + points:(part + 1) * depth, lanes] = rest


def row_of(block, r, rows):
    return block[pl.ds(r, block.shape[0] // rows, stride=rows), :]


def prepare_kernel(peers, pair_count, points, row_points, factor):
    rows, _, tall, depth = factor.shape
    set_index = lax.axis_index("set")
    start = set_index * points
    beside = (set_index ^ 1) * points - start
    slot = lax.broadcasted_iota(jnp.int32, (1, depth), 1)
    point = jnp.where(slot < round_up(points, 128), start + slot, beside)
    heads = round_up(peers + 1, GROUP)
    sub = lax.broadcasted_iota(jnp.int32, (tall, 1), 0)
    order = sub - GROUP
    head = jnp.where(order < peers, (set_index ^ (2 * order)) * pair_count, TRUNC)
    multiplier = jnp.where(sub < GROUP, sub, jnp.where(order < heads, head, (order - heads) * GROUP))
    for r in range(rows):
        length = row_points[r].astype(F32)
        factor[r, 0], factor[r, 1] = unit_circle(multiplier, point, length, 1.0 / length)


def prepare(row_points, points, peers, pair_count):
    rows = row_points.shape[0]
    tall = GROUP + round_up(peers + 1, GROUP) + round_up(pl.cdiv(pair_count, GROUP), GROUP)
    return pl.pallas_call(
        functools.partial(prepare_kernel, peers, pair_count, points),
        out_shape=jax.ShapeDtypeStruct((rows, 2, tall, round_up(points, 128) + 128), F32),
        in_specs=[pl.BlockSpec(memory_space=pltpu.SMEM)],
        out_specs=pl.BlockSpec(memory_space=pltpu.VMEM),
        compiler_params=pltpu.CompilerParams(vmem_limit_bytes=VMEM),
        cost_estimate=micros(1),
        name="prepare",
    )(row_points)


def fourier_kernel(groups, first_group, peers, pair_count, row_points, factor, mine, theirs, *refs):
    outs = refs[:peers]
    values, table, sums, twist, bases = refs[peers:]
    rows = table.shape[0]
    width = outs[0].shape[1]
    depth = table.shape[2] // 3
    held = round_up(pl.cdiv(pair_count, GROUP), GROUP)
    tail = factor.shape[2] - held
    last_at = GROUP + peers
    set_index = lax.axis_index("set")
    points = mine.shape[0] // rows
    for side, block in enumerate((mine, theirs)):
        for r in range(rows):
            store_values(values, r, side, row_of(block, r, rows), (set_index ^ side) * points, row_points[r])
    lane = lax.broadcasted_iota(jnp.int32, (1, width), 1)
    north = lane < width // 2
    sub = lax.broadcasted_iota(jnp.int32, (GROUP, 1), 0)
    for r in range(rows):
        near = factor[r, 0, :GROUP, :], factor[r, 1, :GROUP, :]
        last = factor[r, 0, last_at:last_at + 1, :], factor[r, 1, last_at:last_at + 1, :]
        for peer in range(peers):
            at = GROUP + peer
            head = factor[r, 0, at:at + 1, :], factor[r, 1, at:at + 1, :]
            base = rotate(head, (factor[r, 0, tail:, :], factor[r, 1, tail:, :]))
            bases[r, 0, peer * held:(peer + 1) * held, :] = base[0]
            bases[r, 1, peer * held:(peer + 1) * held, :] = base[1]
        for index in range(peers * groups):
            at = index // groups * held + first_group + index % groups
            base = bases[r, 0, at:at + 1, :], bases[r, 1, at:at + 1, :]
            first = rotate(base, near)
            second = rotate(last, (first[0], -first[1]))
            block = jnp.concatenate([*first, *second], axis=0)
            high, low = split(block[:, :depth])
            lines = slice(index * 4 * GROUP, (index + 1) * 4 * GROUP)
            for part, piece in enumerate((high, high, low)):
                table[r, lines, part * depth:(part + 1) * depth] = piece
            twist[r, lines, :] = block[:, depth:]
        sums[r] = jnp.dot(table[r], values[r], preferred_element_type=F32)
    for peer in range(peers):
        for g in range(groups):
            base = (set_index ^ (2 * peer)) * pair_count + (first_group + g) * GROUP
            for side in range(2):
                wave = base + sub
                wave = TRUNC - wave if side else wave
                at = ((peer * groups + g) * 2 + side) * 2 * GROUP
                for r in range(rows):
                    turn = twist[r, at:at + GROUP, :], twist[r, at + GROUP:at + 2 * GROUP, :]
                    far = sums[r, at:at + GROUP, width:], sums[r, at + GROUP:at + 2 * GROUP, width:]
                    far = rotate(turn, far)
                    real = sums[r, at:at + GROUP, :width] + far[0]
                    imag = sums[r, at + GROUP:at + 2 * GROUP, :width] + far[1]
                    usable = wave <= (row_points[r] - 1) // 2
                    even = jnp.where(north, real, pltpu.roll(imag, width // 2, 1))
                    odd = jnp.where(north, pltpu.roll(real, width // 2, 1), imag)
                    for parity, block in enumerate((even, odd)):
                        to = (((g * 2 + side) * 2 + parity) * rows + r) * GROUP
                        outs[peer][to:to + GROUP, :] = jnp.where(usable, block, 0.0)


def fourier_sums(row_points, factor, mine, theirs, groups, first_group, peers, pair_count):
    rows = row_points.shape[0]
    depth = factor.shape[3] - 128
    width = mine.shape[1]
    out_rows = groups * 4 * rows * GROUP
    tall = peers * groups * 4 * GROUP
    vmem = pl.BlockSpec(memory_space=pltpu.VMEM)
    return pl.pallas_call(
        functools.partial(fourier_kernel, groups, first_group, peers, pair_count),
        out_shape=[jax.ShapeDtypeStruct((out_rows, width), F32)] * peers,
        in_specs=[pl.BlockSpec(memory_space=pltpu.SMEM)] + [vmem] * 3,
        out_specs=[vmem] * peers,
        scratch_shapes=[
            pltpu.VMEM((rows, 3 * depth, 2 * width), BF16),
            pltpu.VMEM((rows, tall, 3 * depth), BF16),
            pltpu.VMEM((rows, tall, 2 * width), F32),
            pltpu.VMEM((rows, tall, 128), F32),
            pltpu.VMEM((rows, 2, peers * round_up(pl.cdiv(pair_count, GROUP), GROUP), depth + 128), F32),
        ],
        compiler_params=pltpu.CompilerParams(vmem_limit_bytes=VMEM),
        cost_estimate=micros(3),
        name="fourier_sums",
    )(row_points, factor, mine, theirs)


def weights_kernel(rows, bands, legend, out):
    pair_count, total, slots = legend.shape
    wide = out.shape[2]
    band_index = lax.axis_index("band")
    first_pair = lax.axis_index("set") * pair_count
    source = lax.broadcasted_iota(jnp.int32, (GROUP * total, 1), 0)
    lane = lax.broadcasted_iota(jnp.int32, (1, wide), 1)
    member = lane % GROUP
    row = lane // GROUP % rows
    parity = lane // (GROUP * rows) % 2
    side = lane // (GROUP * rows * 2) % 2
    band = (lane // (GROUP * rows * 4)) ^ band_index
    spread = (source == member * total + band * rows + row).astype(F32).astype(BF16)
    slot = band_index * slots + lax.broadcasted_iota(jnp.int32, (slots, 1), 0)
    for group in range(out.shape[0]):
        count = min(GROUP, pair_count - group * GROUP)
        held = legend[group * GROUP:group * GROUP + count].astype(F32).reshape(count * total, slots)
        if count < GROUP:
            held = jnp.concatenate([held, jnp.zeros(((GROUP - count) * total, slots), F32)], axis=0)
        moved = lax.dot_general(
            held.astype(BF16), spread, (((0,), (0,)), ((), ())), preferred_element_type=F32
        )
        first = TRUNC - (first_pair + group * GROUP + member)
        start = jnp.where(side == 0, 0, first + 1)
        sign = 1 - 2 * side
        match = (((slot - start) & 1) == parity) & (sign * slot <= sign * first - side)
        out[group] = jnp.where(match, moved, 0.0).astype(BF16)


def spread_weights(legend, rows, bands):
    pair_count, total, slots = legend.shape
    groups = pl.cdiv(pair_count, GROUP)
    vmem = pl.BlockSpec(memory_space=pltpu.VMEM)
    return pl.pallas_call(
        functools.partial(weights_kernel, rows, bands),
        out_shape=jax.ShapeDtypeStruct((groups, slots, bands * 4 * rows * GROUP), BF16),
        in_specs=[vmem],
        out_specs=vmem,
        compiler_params=pltpu.CompilerParams(vmem_limit_bytes=VMEM),
        cost_estimate=micros(1),
        name="spread_weights",
    )(legend)


def spectra_kernel(bands, first_group, pairs, weights, *refs):
    held = refs[:bands]
    out, block, sems = refs[-3:]
    width = held[0].shape[1]
    tall = held[0].shape[0]
    groups = pl.cdiv(pairs, GROUP)
    part = tall // groups
    member = lax.broadcasted_iota(jnp.int32, (2 * GROUP, width), 0) % GROUP
    masks = [jnp.tile((member == i).astype(F32).astype(BF16), (bands * part // (2 * GROUP), 1)) for i in range(GROUP)]
    copies = []
    for g in range(groups):
        stacked = jnp.concatenate([ref[g * part:(g + 1) * part, :] for ref in held], axis=0)
        for at in range(0, min(GROUP, pairs - g * GROUP), 2):
            both = jnp.concatenate([stacked * masks[at], stacked * masks[at + 1]], axis=1)
            product = jnp.dot(weights[first_group + g], both, preferred_element_type=F32)
            pair = g * GROUP + at
            block[pair] = product[:, :width]
            block[pair + 1] = product[:, width:]
            copy = pltpu.make_async_copy(
                block.at[pl.ds(pair, 2)], out.at[pl.ds(first_group * GROUP + pair, 2)], sems.at[pair // 2]
            )
            copy.start()
            copies.append(copy)
    for copy in copies:
        copy.wait()


def spectra_part(weights, held, out, pair_count, first_group, groups):
    bands = len(held)
    width = held[0].shape[1]
    slots = weights.shape[1]
    pairs = min(groups * GROUP, pair_count - first_group * GROUP)
    previous = [] if out is None else [out]
    vmem = pl.BlockSpec(memory_space=pltpu.VMEM)
    anywhere = pl.BlockSpec(memory_space=pl.ANY)
    return pl.pallas_call(
        functools.partial(spectra_kernel, bands, first_group, pairs),
        out_shape=jax.ShapeDtypeStruct((pair_count, slots, width), F32),
        in_specs=[vmem] * (1 + bands) + [anywhere] * len(previous),
        out_specs=anywhere,
        input_output_aliases={1 + bands: 0} if previous else {},
        scratch_shapes=[pltpu.VMEM((pairs, slots, width), F32), pltpu.SemaphoreType.DMA((pairs // 2,))],
        compiler_params=pltpu.CompilerParams(vmem_limit_bytes=VMEM),
        cost_estimate=micros(3),
        name="spectra_part",
    )(weights, *held, *previous)


def swap(axis, size, step):
    return [(i, i ^ step) for i in range(size)]


def exchange(array, axis, steps):
    return [lax.ppermute(part, axis, swap(axis, lax.axis_size(axis), step)) for part, step in zip(array, steps)]


def shards(grid, row_points, legendre):
    set_size = lax.axis_size("set")
    band_size = lax.axis_size("band")
    rows, points, width = grid.shape
    pair_count = legendre.shape[0]
    slots = legendre.shape[2] // band_size
    peers = set_size // 2
    flat = grid.transpose(1, 0, 2).reshape(points * rows, width)
    theirs = lax.ppermute(flat, "set", swap("set", set_size, 1))
    factor = prepare(row_points, points, peers, pair_count)
    legend = lax.dynamic_slice_in_dim(legendre, lax.axis_index("band") * slots, slots, 2)
    legend, theirs = lax.optimization_barrier((legend, theirs))
    weights = spread_weights(legend, rows, band_size)
    all_groups = pl.cdiv(pair_count, GROUP)
    cut = (all_groups + 1) // 2
    chunks = ((0, cut), (cut, all_groups - cut))
    gathered = []
    partial = []
    for first_group, groups in chunks:
        partial.append(fourier_sums(row_points, factor, flat, theirs, groups, first_group, peers, pair_count))
    for parts in partial:
        steps = list(range(1, peers))
        steps = steps[::-1] if gathered else steps[::2] + steps[1::2]
        arrived = exchange([parts[k].astype(WIRE) for k in steps], "set", [2 * k for k in steps])
        if gathered:
            arrived, weights = lax.optimization_barrier((arrived, weights))
        total = parts[0]
        for part in arrived:
            total = total + part.astype(F32)
        rounded = total.astype(BF16)
        turns = list(range(1, band_size))
        gathered.append([rounded] + exchange([rounded] * len(turns), "band", turns))
    out = None
    for held, (first_group, groups) in zip(gathered, chunks):
        out = spectra_part(weights, held, out, pair_count, first_group, groups)
    return out


def solution(mesh):
    return jax.shard_map(
        shards,
        mesh=mesh,
        in_specs=(P("band", "set", None), P("band"), P("set", None, None)),
        out_specs=P("set", "band", None),
        check_vma=False,
    )
```

```python
import functools
import math

import jax
import jax.numpy as jnp
from jax import lax
from jax.experimental import pallas as pl
from jax.experimental.pallas import tpu as pltpu
from jax.sharding import PartitionSpec as P

TRUNC = 1279
GROUP = 8
F32 = jnp.float32
BF16 = jnp.bfloat16
WIRE = jnp.float16
VMEM = 16 * 2**20


def round_up(value, step):
    return -(-value // step) * step


def unit_circle(multiplier, point, length, inverse):
    product = (multiplier * point).astype(F32)
    residue = product - jnp.floor(product * inverse + 0.5) * length
    quarters = 4.0 * residue * inverse
    turn = jnp.floor(quarters + 0.5)
    angle = (quarters - turn) * (0.5 * math.pi)
    square = angle * angle
    sine = angle * (1.0 + square * (-1 / 6 + square * (1 / 120 + square * (-1 / 5040 + square / 362880))))
    cosine = 1.0 + square * (-0.5 + square * (1 / 24 + square * (-1 / 720 + square / 40320)))
    quadrant = turn.astype(jnp.int32) & 3
    odd = (quadrant & 1) == 1
    real = jnp.where(odd, sine, cosine)
    imag = jnp.where(odd, cosine, sine)
    real = jnp.where((quadrant == 1) | (quadrant == 2), -real, real)
    imag = jnp.where(quadrant >= 2, imag, -imag)
    return real, imag


def micros(count):
    return pl.CostEstimate(flops=0, bytes_accessed=count * 3 * 10**6, transcendentals=0)


def rotate(a, b):
    return a[0] * b[0] - a[1] * b[1], a[0] * b[1] + a[1] * b[0]


def split(values):
    high = values.astype(BF16)
    return high, (values - high.astype(F32)).astype(BF16)


def layout(points):
    rest = points % 128
    return points - rest, rest, round_up(3 * rest, 128)


def store_values(out, side, raw, start, length):
    points, width = raw.shape
    body, rest, extra = layout(points)
    lane = lax.broadcasted_iota(jnp.int32, (1, width), 1)
    sign = jnp.where(lane < width // 2, 1.0, -1.0)
    where = start + lax.broadcasted_iota(jnp.int32, (points, 1), 0)
    folded = pltpu.roll(raw, width // 2, 1) + raw * sign
    folded = jnp.where(where.astype(F32) < length, folded, 0.0)
    lanes = slice(side * width, (side + 1) * width)
    high, low = split(folded[:body])
    for part, piece in enumerate((high, low, high)):
        out[part * body:(part + 1) * body, lanes] = piece
    if rest:
        high, low = split(folded[body:])
        parts = [piece.astype(F32) for piece in (high, low, high)]
        parts.append(jnp.zeros((extra - 3 * rest, width), F32))
        out[3 * body:, lanes] = jnp.concatenate(parts, axis=0).astype(BF16)


def row_of(block, r, rows):
    return block[pl.ds(r, block.shape[0] // rows, stride=rows), :]


def prepare_kernel(peers, pair_count, points, row_points, factor):
    rows, _, tall, wide = factor.shape
    body, rest, extra = layout(points)
    set_index = lax.axis_index("set")
    start = set_index * points
    beside = (set_index ^ 1) * points - start
    slot = lax.broadcasted_iota(jnp.int32, (1, wide), 1)
    point = start + jnp.where(slot < body, slot, body + (slot - body) % max(rest, 1))
    point = jnp.where(slot < body + extra, point, beside)
    heads = round_up(peers + 1, GROUP)
    sub = lax.broadcasted_iota(jnp.int32, (tall, 1), 0)
    order = sub - GROUP
    head = jnp.where(order < peers, (set_index ^ (2 * order)) * pair_count, TRUNC)
    multiplier = jnp.where(sub < GROUP, sub, jnp.where(order < heads, head, (order - heads) * GROUP))
    for r in range(rows):
        length = row_points[r].astype(F32)
        scale = jnp.where(slot < body + extra, lax.rsqrt(jnp.full((1, wide), length, F32)), 1.0)
        scale = jnp.where(sub < GROUP, scale, 1.0)
        real, imag = unit_circle(multiplier, point, length, 1.0 / length)
        factor[r, 0] = jnp.where(order == heads - 1, length, real * scale)
        factor[r, 1] = imag * scale


def table_rows(peers, pair_count):
    return GROUP + round_up(peers + 2, GROUP), round_up(pl.cdiv(pair_count, GROUP), GROUP)


def prepare(row_points, points, peers, pair_count):
    rows = row_points.shape[0]
    body, _, extra = layout(points)
    return pl.pallas_call(
        functools.partial(prepare_kernel, peers, pair_count, points),
        out_shape=jax.ShapeDtypeStruct((rows, 2, sum(table_rows(peers, pair_count)), body + extra + 128), F32),
        in_specs=[pl.BlockSpec(memory_space=pltpu.SMEM)],
        out_specs=pl.BlockSpec(memory_space=pltpu.VMEM),
        compiler_params=pltpu.CompilerParams(vmem_limit_bytes=VMEM),
        cost_estimate=micros(1),
        name="prepare",
    )(row_points)


def fourier_kernel(groups, first_group, peers, pair_count, factor, mine, theirs, *refs):
    outs = refs[:peers]
    rows = factor.shape[0]
    scratch = refs[peers:]
    points = mine.shape[0] // rows
    width = mine.shape[1]
    body, rest, extra = layout(points)
    tail, _ = table_rows(peers, pair_count)
    last_at = GROUP + peers
    set_index = lax.axis_index("set")
    sub = lax.broadcasted_iota(jnp.int32, (GROUP, 1), 0)
    whole = lax.broadcasted_iota(jnp.int32, (1, extra), 1) < 2 * rest
    size = 4 * GROUP * groups
    for r in range(rows):
        values, table, sums, twist = scratch[4 * r:4 * r + 4]
        length = factor[r, 0, tail - 1:tail, :width]
        for side, block in enumerate((mine, theirs)):
            store_values(values, side, row_of(block, r, rows), (set_index ^ side) * points, length)
        near = factor[r, 0, :GROUP, :], factor[r, 1, :GROUP, :]
        last = factor[r, 0, last_at:last_at + 1, :], factor[r, 1, last_at:last_at + 1, :]
        for peer in range(peers):
            at = GROUP + peer
            head = factor[r, 0, at:at + 1, :], factor[r, 1, at:at + 1, :]
            for g in range(groups):
                at = tail + first_group + g
                base = rotate(head, (factor[r, 0, at:at + 1, :], factor[r, 1, at:at + 1, :]))
                first = rotate(base, near)
                second = rotate(last, (first[0], -first[1]))
                block = jnp.concatenate([*first, *second], axis=0)
                lines = slice(peer * size + g * 4 * GROUP, peer * size + (g + 1) * 4 * GROUP)
                high, low = split(block[:, :body])
                for part, piece in enumerate((high, high, low)):
                    table[lines, part * body:(part + 1) * body] = piece
                if rest:
                    end = block[:, body:body + extra]
                    end = jnp.where(whole, end, end - end.astype(BF16).astype(F32))
                    table[lines, 3 * body:] = end.astype(BF16)
                twist[lines, :] = block[:, body + extra:]
        sums[...] = jnp.dot(table[...], values[...], preferred_element_type=F32)
    for r in range(rows):
        values, table, sums, twist = scratch[4 * r:4 * r + 4]
        length = factor[r, 0, tail - 1:tail, :width]
        for peer in range(peers):
            for g in range(groups):
                base = (set_index ^ (2 * peer)) * pair_count + (first_group + g) * GROUP
                for side in range(2):
                    wave = base + sub
                    wave = TRUNC - wave if side else wave
                    usable = (2 * wave + 1).astype(F32) <= length
                    at = ((peer * groups + g) * 2 + side) * 2 * GROUP
                    real, imag = slice(at, at + GROUP), slice(at + GROUP, at + 2 * GROUP)
                    far = rotate((twist[real, :], twist[imag, :]), (sums[real, width:], sums[imag, width:]))
                    for e, lines in enumerate((real, imag)):
                        to = (((g * 2 + side) * 2 + e) * rows + r) * GROUP
                        outs[peer][to:to + GROUP, :] = jnp.where(usable, sums[lines, :width] + far[e], 0.0)


def fourier_sums(factor, mine, theirs, groups, first_group, peers, pair_count):
    rows = factor.shape[0]
    width = mine.shape[1]
    body, _, extra = layout(mine.shape[0] // rows)
    out_rows = groups * 4 * rows * GROUP
    tall = peers * groups * 4 * GROUP
    vmem = pl.BlockSpec(memory_space=pltpu.VMEM)
    return pl.pallas_call(
        functools.partial(fourier_kernel, groups, first_group, peers, pair_count),
        out_shape=[jax.ShapeDtypeStruct((out_rows, width), F32)] * peers,
        in_specs=[vmem] * 3,
        out_specs=[vmem] * peers,
        scratch_shapes=[
            pltpu.VMEM((3 * body + extra, 2 * width), BF16),
            pltpu.VMEM((tall, 3 * body + extra), BF16),
            pltpu.VMEM((tall, 2 * width), F32),
            pltpu.VMEM((tall, 128), F32),
        ] * rows,
        compiler_params=pltpu.CompilerParams(vmem_limit_bytes=VMEM),
        cost_estimate=micros(3),
        name="fourier_sums",
    )(factor, mine, theirs)


def weights_kernel(rows, bands, legend, out):
    pair_count, total, slots = legend.shape
    wide = out.shape[2]
    band_index = lax.axis_index("band")
    first_pair = lax.axis_index("set") * pair_count
    source = lax.broadcasted_iota(jnp.int32, (GROUP * total, 1), 0)
    lane = lax.broadcasted_iota(jnp.int32, (1, wide), 1)
    member = lane % GROUP
    row = lane // GROUP % rows
    parity = lane // (GROUP * rows) % 2
    side = lane // (GROUP * rows * 2) % 2
    band = (lane // (GROUP * rows * 4)) ^ band_index
    spread = (source == member * total + band * rows + row).astype(F32).astype(BF16)
    slot = band_index * slots + lax.broadcasted_iota(jnp.int32, (slots, 1), 0)
    for group in range(out.shape[0]):
        count = min(GROUP, pair_count - group * GROUP)
        held = legend[group * GROUP:group * GROUP + count].astype(F32).reshape(count * total, slots)
        if count < GROUP:
            held = jnp.concatenate([held, jnp.zeros(((GROUP - count) * total, slots), F32)], axis=0)
        moved = lax.dot_general(
            held.astype(BF16), spread, (((0,), (0,)), ((), ())), preferred_element_type=F32
        )
        first = TRUNC - (first_pair + group * GROUP + member)
        start = jnp.where(side == 0, 0, first + 1)
        sign = 1 - 2 * side
        match = (((slot - start) & 1) == parity) & (sign * slot <= sign * first - side)
        out[group] = jnp.where(match, moved, 0.0).astype(BF16)


def spread_weights(legend, rows, bands):
    pair_count, total, slots = legend.shape
    groups = pl.cdiv(pair_count, GROUP)
    vmem = pl.BlockSpec(memory_space=pltpu.VMEM)
    return pl.pallas_call(
        functools.partial(weights_kernel, rows, bands),
        out_shape=jax.ShapeDtypeStruct((groups, slots, bands * 4 * rows * GROUP), BF16),
        in_specs=[vmem],
        out_specs=vmem,
        compiler_params=pltpu.CompilerParams(vmem_limit_bytes=VMEM),
        cost_estimate=micros(1),
        name="spread_weights",
    )(legend)


def arrange(block):
    width = block.shape[1]
    tall = block.shape[0] // 4
    north = lax.broadcasted_iota(jnp.int32, (1, width), 1) < width // 2
    done = []
    for side in range(2):
        real = block[2 * side * tall:(2 * side + 1) * tall, :].astype(F32)
        imag = block[(2 * side + 1) * tall:(2 * side + 2) * tall, :].astype(F32)
        done.append(jnp.where(north, real, pltpu.roll(imag, width // 2, 1)))
        done.append(jnp.where(north, pltpu.roll(real, width // 2, 1), imag))
    return jnp.concatenate(done, axis=0).astype(BF16)


def spectra_kernel(bands, first_group, pairs, weights, *refs):
    held = refs[:bands]
    out, block, sems = refs[-3:]
    width = held[0].shape[1]
    tall = held[0].shape[0]
    groups = pl.cdiv(pairs, GROUP)
    part = tall // groups
    member = lax.broadcasted_iota(jnp.int32, (2 * GROUP, width), 0) % GROUP
    masks = [jnp.tile((member == i).astype(F32).astype(BF16), (bands * part // (2 * GROUP), 1)) for i in range(GROUP)]
    copies = []
    for g in range(groups):
        stacked = jnp.concatenate([arrange(ref[g * part:(g + 1) * part, :]) for ref in held], axis=0)
        for at in range(0, min(GROUP, pairs - g * GROUP), 2):
            both = jnp.concatenate([stacked * masks[at], stacked * masks[at + 1]], axis=1)
            product = jnp.dot(weights[first_group + g], both, preferred_element_type=F32)
            pair = g * GROUP + at
            block[pair] = product[:, :width]
            block[pair + 1] = product[:, width:]
            copy = pltpu.make_async_copy(
                block.at[pl.ds(pair, 2)], out.at[pl.ds(first_group * GROUP + pair, 2)], sems.at[pair // 2]
            )
            copy.start()
            copies.append(copy)
    for copy in copies:
        copy.wait()


def spectra_part(weights, held, out, pair_count, first_group, groups):
    bands = len(held)
    width = held[0].shape[1]
    slots = weights.shape[1]
    pairs = min(groups * GROUP, pair_count - first_group * GROUP)
    previous = [] if out is None else [out]
    vmem = pl.BlockSpec(memory_space=pltpu.VMEM)
    anywhere = pl.BlockSpec(memory_space=pl.ANY)
    return pl.pallas_call(
        functools.partial(spectra_kernel, bands, first_group, pairs),
        out_shape=jax.ShapeDtypeStruct((pair_count, slots, width), F32),
        in_specs=[vmem] * (1 + bands) + [anywhere] * len(previous),
        out_specs=anywhere,
        input_output_aliases={1 + bands: 0} if previous else {},
        scratch_shapes=[pltpu.VMEM((pairs, slots, width), F32), pltpu.SemaphoreType.DMA((pairs // 2,))],
        compiler_params=pltpu.CompilerParams(vmem_limit_bytes=VMEM),
        cost_estimate=micros(3),
        name="spectra_part",
    )(weights, *held, *previous)


def swap(axis, size, step):
    return [(i, i ^ step) for i in range(size)]


def exchange(array, axis, steps):
    return [lax.ppermute(part, axis, swap(axis, lax.axis_size(axis), step)) for part, step in zip(array, steps)]


def shards(grid, row_points, legendre):
    set_size = lax.axis_size("set")
    band_size = lax.axis_size("band")
    rows, points, width = grid.shape
    pair_count = legendre.shape[0]
    slots = legendre.shape[2] // band_size
    peers = set_size // 2
    flat = grid.transpose(1, 0, 2).reshape(points * rows, width)
    theirs = lax.ppermute(flat, "set", swap("set", set_size, 1))
    factor = prepare(row_points, points, peers, pair_count)
    legend = lax.dynamic_slice_in_dim(legendre, lax.axis_index("band") * slots, slots, 2)
    legend, theirs = lax.optimization_barrier((legend, theirs))
    weights = None
    all_groups = pl.cdiv(pair_count, GROUP)
    cut = (all_groups + 1) // 2
    chunks = ((0, cut), (cut, all_groups - cut))
    gathered = []
    partial = []
    for first_group, groups in chunks:
        partial.append(fourier_sums(factor, flat, theirs, groups, first_group, peers, pair_count))
    for parts in partial:
        steps = list(range(1, peers))
        steps = steps[::-1] if gathered else steps[::2] + steps[1::2]
        arrived = exchange([parts[k].astype(WIRE) for k in steps], "set", [2 * k for k in steps])
        if gathered:
            arrived, weights = lax.optimization_barrier((arrived, weights))
        total = parts[0]
        for part in arrived:
            total = total + part.astype(F32)
        rounded = total.astype(BF16)
        if not gathered:
            legend, rounded = lax.optimization_barrier((legend, rounded))
            weights = spread_weights(legend, rows, band_size)
        turns = list(range(1, band_size))
        gathered.append([rounded] + exchange([rounded] * len(turns), "band", turns))
    out = None
    for held, (first_group, groups) in zip(gathered, chunks):
        out = spectra_part(weights, held, out, pair_count, first_group, groups)
    return out


def solution(mesh):
    return jax.shard_map(
        shards,
        mesh=mesh,
        in_specs=(P("band", "set", None), P("band"), P("set", None, None)),
        out_specs=P("set", "band", None),
        check_vma=False,
    )
```

```python
import functools
import math

import jax
import jax.numpy as jnp
from jax import lax
from jax.experimental import pallas as pl
from jax.experimental.pallas import tpu as pltpu
from jax.sharding import PartitionSpec as P

TRUNC = 1279
GROUP = 8
F32 = jnp.float32
BF16 = jnp.bfloat16
WIRE = jnp.float16
VMEM = 16 * 2**20


def round_up(value, step):
    return -(-value // step) * step


def unit_circle(multiplier, point, length, inverse):
    product = (multiplier * point).astype(F32)
    residue = product - jnp.floor(product * inverse + 0.5) * length
    quarters = 4.0 * residue * inverse
    turn = jnp.floor(quarters + 0.5)
    angle = (quarters - turn) * (0.5 * math.pi)
    square = angle * angle
    sine = angle * (1.0 + square * (-1 / 6 + square * (1 / 120 + square * (-1 / 5040 + square / 362880))))
    cosine = 1.0 + square * (-0.5 + square * (1 / 24 + square * (-1 / 720 + square / 40320)))
    quadrant = turn.astype(jnp.int32) & 3
    odd = (quadrant & 1) == 1
    real = jnp.where(odd, sine, cosine)
    imag = jnp.where(odd, cosine, sine)
    real = jnp.where((quadrant == 1) | (quadrant == 2), -real, real)
    imag = jnp.where(quadrant >= 2, imag, -imag)
    return real, imag


def micros(count):
    return pl.CostEstimate(flops=0, bytes_accessed=count * 3 * 10**6, transcendentals=0)


def rotate(a, b):
    return a[0] * b[0] - a[1] * b[1], a[0] * b[1] + a[1] * b[0]


def split(values):
    high = values.astype(BF16)
    return high, (values - high.astype(F32)).astype(BF16)


def layout(points):
    rest = points % 128
    return points - rest, rest, round_up(3 * rest, 128)


def store_values(out, side, raw, start, length):
    points, width = raw.shape
    body, rest, extra = layout(points)
    lane = lax.broadcasted_iota(jnp.int32, (1, width), 1)
    sign = jnp.where(lane < width // 2, 1.0, -1.0)
    where = start + lax.broadcasted_iota(jnp.int32, (points, 1), 0)
    folded = pltpu.roll(raw, width // 2, 1) + raw * sign
    folded = jnp.where(where.astype(F32) < length, folded, 0.0)
    lanes = slice(side * width, (side + 1) * width)
    high, low = split(folded[:body])
    for part, piece in enumerate((high, low, high)):
        out[part * body:(part + 1) * body, lanes] = piece
    if rest:
        high, low = split(folded[body:])
        parts = [piece.astype(F32) for piece in (high, low, high)]
        parts.append(jnp.zeros((extra - 3 * rest, width), F32))
        out[3 * body:, lanes] = jnp.concatenate(parts, axis=0).astype(BF16)


def row_of(block, r, rows):
    return block[pl.ds(r, block.shape[0] // rows, stride=rows), :]


def prepare_kernel(peers, pair_count, points, row_points, factor):
    rows, _, tall, wide = factor.shape
    body, rest, extra = layout(points)
    set_index = lax.axis_index("set")
    start = set_index * points
    beside = (set_index ^ 1) * points - start
    slot = lax.broadcasted_iota(jnp.int32, (1, wide), 1)
    point = start + jnp.where(slot < body, slot, body + (slot - body) % max(rest, 1))
    point = jnp.where(slot < body + extra, point, beside)
    heads = peers + 2
    sub = lax.broadcasted_iota(jnp.int32, (tall, 1), 0)
    order = sub - GROUP
    head = jnp.where(order < peers, (set_index ^ (2 * order)) * pair_count, TRUNC)
    multiplier = jnp.where(sub < GROUP, sub, jnp.where(order < heads, head, (order - heads) * GROUP))
    for r in range(rows):
        length = row_points[r].astype(F32)
        scale = jnp.where(slot < body + extra, lax.rsqrt(jnp.full((1, wide), length, F32)), 1.0)
        scale = jnp.where(sub < GROUP, scale, 1.0)
        real, imag = unit_circle(multiplier, point, length, 1.0 / length)
        factor[r, 0] = jnp.where(order == heads - 1, length, real * scale)
        factor[r, 1] = imag * scale


def table_rows(peers, pair_count):
    heads, groups = peers + 2, pl.cdiv(pair_count, GROUP)
    return GROUP + heads, round_up(heads + groups, GROUP) - heads


def prepare(row_points, points, peers, pair_count):
    rows = row_points.shape[0]
    body, _, extra = layout(points)
    return pl.pallas_call(
        functools.partial(prepare_kernel, peers, pair_count, points),
        out_shape=jax.ShapeDtypeStruct((rows, 2, sum(table_rows(peers, pair_count)), body + extra + 128), F32),
        in_specs=[pl.BlockSpec(memory_space=pltpu.SMEM)],
        out_specs=pl.BlockSpec(memory_space=pltpu.VMEM),
        compiler_params=pltpu.CompilerParams(vmem_limit_bytes=VMEM),
        cost_estimate=micros(1),
        name="prepare",
    )(row_points)


def fourier_kernel(groups, first_group, peers, pair_count, factor, mine, theirs, *refs):
    outs = refs[:peers]
    rows = factor.shape[0]
    scratch = refs[peers:]
    points = mine.shape[0] // rows
    width = mine.shape[1]
    body, rest, extra = layout(points)
    tail, _ = table_rows(peers, pair_count)
    last_at = GROUP + peers
    set_index = lax.axis_index("set")
    sub = lax.broadcasted_iota(jnp.int32, (GROUP, 1), 0)
    whole = lax.broadcasted_iota(jnp.int32, (1, extra), 1) < 2 * rest
    size = 4 * GROUP * groups
    for r in range(rows):
        values, table, sums, twist = scratch[4 * r:4 * r + 4]
        length = factor[r, 0, tail - 1:tail, :width]
        for side, block in enumerate((mine, theirs)):
            store_values(values, side, row_of(block, r, rows), (set_index ^ side) * points, length)
        near = factor[r, 0, :GROUP, :], factor[r, 1, :GROUP, :]
        last = factor[r, 0, last_at:last_at + 1, :], factor[r, 1, last_at:last_at + 1, :]
        for peer in range(peers):
            at = GROUP + peer
            head = factor[r, 0, at:at + 1, :], factor[r, 1, at:at + 1, :]
            for g in range(groups):
                at = tail + first_group + g
                base = rotate(head, (factor[r, 0, at:at + 1, :], factor[r, 1, at:at + 1, :]))
                first = rotate(base, near)
                second = rotate(last, (first[0], -first[1]))
                block = jnp.concatenate([*first, *second], axis=0)
                lines = slice(peer * size + g * 4 * GROUP, peer * size + (g + 1) * 4 * GROUP)
                high, low = split(block[:, :body])
                for part, piece in enumerate((high, high, low)):
                    table[lines, part * body:(part + 1) * body] = piece
                if rest:
                    end = block[:, body:body + extra]
                    end = jnp.where(whole, end, end - end.astype(BF16).astype(F32))
                    table[lines, 3 * body:] = end.astype(BF16)
                twist[lines, :] = block[:, body + extra:]
        sums[...] = jnp.dot(table[...], values[...], preferred_element_type=F32)
    for r in range(rows):
        values, table, sums, twist = scratch[4 * r:4 * r + 4]
        length = factor[r, 0, tail - 1:tail, :width]
        for peer in range(peers):
            for g in range(groups):
                base = (set_index ^ (2 * peer)) * pair_count + (first_group + g) * GROUP
                for side in range(2):
                    wave = base + sub
                    wave = TRUNC - wave if side else wave
                    usable = (2 * wave + 1).astype(F32) <= length
                    at = ((peer * groups + g) * 2 + side) * 2 * GROUP
                    real, imag = slice(at, at + GROUP), slice(at + GROUP, at + 2 * GROUP)
                    far = rotate((twist[real, :], twist[imag, :]), (sums[real, width:], sums[imag, width:]))
                    for e, lines in enumerate((real, imag)):
                        to = (((g * 2 + side) * 2 + e) * rows + r) * GROUP
                        outs[peer][to:to + GROUP, :] = jnp.where(usable, sums[lines, :width] + far[e], 0.0)


def fourier_sums(factor, mine, theirs, groups, first_group, peers, pair_count):
    rows = factor.shape[0]
    width = mine.shape[1]
    body, _, extra = layout(mine.shape[0] // rows)
    out_rows = groups * 4 * rows * GROUP
    tall = peers * groups * 4 * GROUP
    vmem = pl.BlockSpec(memory_space=pltpu.VMEM)
    return pl.pallas_call(
        functools.partial(fourier_kernel, groups, first_group, peers, pair_count),
        out_shape=[jax.ShapeDtypeStruct((out_rows, width), F32)] * peers,
        in_specs=[vmem] * 3,
        out_specs=[vmem] * peers,
        scratch_shapes=[
            pltpu.VMEM((3 * body + extra, 2 * width), BF16),
            pltpu.VMEM((tall, 3 * body + extra), BF16),
            pltpu.VMEM((tall, 2 * width), F32),
            pltpu.VMEM((tall, 128), F32),
        ] * rows,
        compiler_params=pltpu.CompilerParams(vmem_limit_bytes=VMEM),
        cost_estimate=micros(3),
        name="fourier_sums",
    )(factor, mine, theirs)


def weights_kernel(rows, bands, legend, out):
    pair_count, total, slots = legend.shape
    wide = out.shape[2]
    band_index = lax.axis_index("band")
    first_pair = lax.axis_index("set") * pair_count
    source = lax.broadcasted_iota(jnp.int32, (GROUP * total, 1), 0)
    lane = lax.broadcasted_iota(jnp.int32, (1, wide), 1)
    member = lane % GROUP
    row = lane // GROUP % rows
    parity = lane // (GROUP * rows) % 2
    side = lane // (GROUP * rows * 2) % 2
    band = (lane // (GROUP * rows * 4)) ^ band_index
    spread = (source == member * total + band * rows + row).astype(F32).astype(BF16)
    slot = band_index * slots + lax.broadcasted_iota(jnp.int32, (slots, 1), 0)
    for group in range(out.shape[0]):
        count = min(GROUP, pair_count - group * GROUP)
        held = legend[group * GROUP:group * GROUP + count].astype(F32).reshape(count * total, slots)
        if count < GROUP:
            held = jnp.concatenate([held, jnp.zeros(((GROUP - count) * total, slots), F32)], axis=0)
        moved = lax.dot_general(
            held.astype(BF16), spread, (((0,), (0,)), ((), ())), preferred_element_type=F32
        )
        first = TRUNC - (first_pair + group * GROUP + member)
        start = jnp.where(side == 0, 0, first + 1)
        sign = 1 - 2 * side
        match = (((slot - start) & 1) == parity) & (sign * slot <= sign * first - side)
        out[group] = jnp.where(match, moved, 0.0).astype(BF16)


def spread_weights(legend, rows, bands):
    pair_count, total, slots = legend.shape
    groups = pl.cdiv(pair_count, GROUP)
    vmem = pl.BlockSpec(memory_space=pltpu.VMEM)
    return pl.pallas_call(
        functools.partial(weights_kernel, rows, bands),
        out_shape=jax.ShapeDtypeStruct((groups, slots, bands * 4 * rows * GROUP), BF16),
        in_specs=[vmem],
        out_specs=vmem,
        compiler_params=pltpu.CompilerParams(vmem_limit_bytes=VMEM),
        cost_estimate=micros(1),
        name="spread_weights",
    )(legend)


def arrange(block):
    width = block.shape[1]
    tall = block.shape[0] // 4
    north = lax.broadcasted_iota(jnp.int32, (1, width), 1) < width // 2
    done = []
    for side in range(2):
        real = block[2 * side * tall:(2 * side + 1) * tall, :].astype(F32)
        imag = block[(2 * side + 1) * tall:(2 * side + 2) * tall, :].astype(F32)
        done.append(jnp.where(north, real, pltpu.roll(imag, width // 2, 1)))
        done.append(jnp.where(north, pltpu.roll(real, width // 2, 1), imag))
    return jnp.concatenate(done, axis=0).astype(BF16)


def spectra_kernel(bands, first_group, pairs, weights, *refs):
    held = refs[:bands]
    out, block, sems = refs[-3:]
    width = held[0].shape[1]
    tall = held[0].shape[0]
    groups = pl.cdiv(pairs, GROUP)
    part = tall // groups
    member = lax.broadcasted_iota(jnp.int32, (2 * GROUP, width), 0) % GROUP
    masks = [jnp.tile((member == i).astype(F32).astype(BF16), (bands * part // (2 * GROUP), 1)) for i in range(GROUP)]
    copies = []
    for g in range(groups):
        stacked = jnp.concatenate([arrange(ref[g * part:(g + 1) * part, :]) for ref in held], axis=0)
        for at in range(0, min(GROUP, pairs - g * GROUP), 2):
            both = jnp.concatenate([stacked * masks[at], stacked * masks[at + 1]], axis=1)
            product = jnp.dot(weights[first_group + g], both, preferred_element_type=F32)
            pair = g * GROUP + at
            block[pair] = product[:, :width]
            block[pair + 1] = product[:, width:]
            copy = pltpu.make_async_copy(
                block.at[pl.ds(pair, 2)], out.at[pl.ds(first_group * GROUP + pair, 2)], sems.at[pair // 2]
            )
            copy.start()
            copies.append(copy)
    for copy in copies:
        copy.wait()


def spectra_part(weights, held, out, pair_count, first_group, groups):
    bands = len(held)
    width = held[0].shape[1]
    slots = weights.shape[1]
    pairs = min(groups * GROUP, pair_count - first_group * GROUP)
    previous = [] if out is None else [out]
    vmem = pl.BlockSpec(memory_space=pltpu.VMEM)
    anywhere = pl.BlockSpec(memory_space=pl.ANY)
    return pl.pallas_call(
        functools.partial(spectra_kernel, bands, first_group, pairs),
        out_shape=jax.ShapeDtypeStruct((pair_count, slots, width), F32),
        in_specs=[vmem] * (1 + bands) + [anywhere] * len(previous),
        out_specs=anywhere,
        input_output_aliases={1 + bands: 0} if previous else {},
        scratch_shapes=[pltpu.VMEM((pairs, slots, width), F32), pltpu.SemaphoreType.DMA((pairs // 2,))],
        compiler_params=pltpu.CompilerParams(vmem_limit_bytes=VMEM),
        cost_estimate=micros(3),
        name="spectra_part",
    )(weights, *held, *previous)


def swap(axis, size, step):
    return [(i, i ^ step) for i in range(size)]


def exchange(array, axis, steps):
    return [lax.ppermute(part, axis, swap(axis, lax.axis_size(axis), step)) for part, step in zip(array, steps)]


def shards(grid, row_points, legendre):
    set_size = lax.axis_size("set")
    band_size = lax.axis_size("band")
    rows, points, width = grid.shape
    pair_count = legendre.shape[0]
    slots = legendre.shape[2] // band_size
    peers = set_size // 2
    flat = grid.transpose(1, 0, 2).reshape(points * rows, width)
    theirs = lax.ppermute(flat, "set", swap("set", set_size, 1))
    factor = prepare(row_points, points, peers, pair_count)
    legend = lax.dynamic_slice_in_dim(legendre, lax.axis_index("band") * slots, slots, 2)
    legend, theirs = lax.optimization_barrier((legend, theirs))
    weights = None
    all_groups = pl.cdiv(pair_count, GROUP)
    cut = (all_groups + 1) // 2
    chunks = ((0, cut), (cut, all_groups - cut))
    gathered = []
    partial = []
    for first_group, groups in chunks:
        partial.append(fourier_sums(factor, flat, theirs, groups, first_group, peers, pair_count))
    for parts in partial:
        steps = list(range(1, peers))
        steps = steps[::-1] if gathered else steps[::2] + steps[1::2]
        arrived = exchange([parts[k].astype(WIRE) for k in steps], "set", [2 * k for k in steps])
        if gathered:
            arrived, weights = lax.optimization_barrier((arrived, weights))
        total = parts[0]
        for part in arrived:
            total = total + part.astype(F32)
        rounded = total.astype(BF16)
        if not gathered:
            legend, rounded = lax.optimization_barrier((legend, rounded))
            weights = spread_weights(legend, rows, band_size)
        turns = list(range(1, band_size))
        gathered.append([rounded] + exchange([rounded] * len(turns), "band", turns))
    out = None
    for held, (first_group, groups) in zip(gathered, chunks):
        out = spectra_part(weights, held, out, pair_count, first_group, groups)
    return out


def solution(mesh):
    return jax.shard_map(
        shards,
        mesh=mesh,
        in_specs=(P("band", "set", None), P("band"), P("set", None, None)),
        out_specs=P("set", "band", None),
        check_vma=False,
    )
```

```python
import functools
import math

import jax
import jax.numpy as jnp
from jax import lax
from jax.experimental import pallas as pl
from jax.experimental.pallas import tpu as pltpu
from jax.sharding import PartitionSpec as P

TRUNC = 1279
GROUP = 8
F32 = jnp.float32
BF16 = jnp.bfloat16
WIRE = jnp.float16
VMEM = 16 * 2**20


def round_up(value, step):
    return -(-value // step) * step


def unit_circle(multiplier, point, length, inverse):
    product = (multiplier * point).astype(F32)
    residue = product - jnp.floor(product * inverse + 0.5) * length
    quarters = 4.0 * residue * inverse
    turn = jnp.floor(quarters + 0.5)
    angle = (quarters - turn) * (0.5 * math.pi)
    square = angle * angle
    sine = angle * (1.0 + square * (-1 / 6 + square * (1 / 120 + square * (-1 / 5040 + square / 362880))))
    cosine = 1.0 + square * (-0.5 + square * (1 / 24 + square * (-1 / 720 + square / 40320)))
    quadrant = turn.astype(jnp.int32) & 3
    odd = (quadrant & 1) == 1
    real = jnp.where(odd, sine, cosine)
    imag = jnp.where(odd, cosine, sine)
    real = jnp.where((quadrant == 1) | (quadrant == 2), -real, real)
    imag = jnp.where(quadrant >= 2, imag, -imag)
    return real, imag


def micros(count):
    return pl.CostEstimate(flops=0, bytes_accessed=count * 3 * 10**6, transcendentals=0)


def rotate(a, b):
    return a[0] * b[0] - a[1] * b[1], a[0] * b[1] + a[1] * b[0]


def split(values):
    high = values.astype(BF16)
    return high, (values - high.astype(F32)).astype(BF16)


def layout(points):
    rest = points % 128
    return points - rest, rest, round_up(3 * rest, 128)


def hemisphere_sign(width):
    return jnp.where(lax.broadcasted_iota(jnp.int32, (1, width), 1) < width // 2, 1.0, -1.0)


def store_values(out, side, raw, start, length):
    points, width = raw.shape
    body, rest, extra = layout(points)
    sign = hemisphere_sign(width)
    where = start + lax.broadcasted_iota(jnp.int32, (points, 1), 0)
    folded = pltpu.roll(raw, width // 2, 1) + raw * sign
    folded = jnp.where(where.astype(F32) < length, folded, 0.0)
    lanes = slice(side * width, (side + 1) * width)
    high, low = split(folded[:body])
    for part, piece in enumerate((high, low, high)):
        out[part * body:(part + 1) * body, lanes] = piece
    if rest:
        high, low = split(folded[body:])
        parts = [piece.astype(F32) for piece in (high, low, high)]
        parts.append(jnp.zeros((extra - 3 * rest, width), F32))
        out[3 * body:, lanes] = jnp.concatenate(parts, axis=0).astype(BF16)


def row_of(block, r, rows, points):
    return block[pl.ds(r, points, stride=rows), :]


def prepare_kernel(peers, pair_count, points, lengths, factor):
    rows, _, tall, wide = factor.shape
    body, rest, extra = layout(points)
    set_index = lax.axis_index("set")
    start = set_index * points
    beside = (set_index ^ 1) * points - start
    slot = lax.broadcasted_iota(jnp.int32, (1, wide), 1)
    point = start + jnp.where(slot < body, slot, body + (slot - body) % max(rest, 1))
    point = jnp.where(slot < body + extra, point, beside)
    heads = peers + 2
    sub = lax.broadcasted_iota(jnp.int32, (tall, 1), 0)
    order = sub - GROUP
    head = jnp.where(order < peers, (set_index ^ (2 * order)) * pair_count, TRUNC)
    multiplier = jnp.where(sub < GROUP, sub, jnp.where(order < heads, head, (order - heads) * GROUP))
    for r in range(rows):
        length = lengths[r:r + 1, :1]
        scale = jnp.where(slot < body + extra, lax.rsqrt(jnp.broadcast_to(length, (1, wide))), 1.0)
        scale = jnp.where(sub < GROUP, scale, 1.0)
        real, imag = unit_circle(multiplier, point, length, 1.0 / length)
        factor[r, 0] = jnp.where(order == heads - 1, length, real * scale)
        factor[r, 1] = imag * scale


def table_rows(peers, pair_count):
    heads, groups = peers + 2, pl.cdiv(pair_count, GROUP)
    return GROUP + heads, round_up(heads + groups, GROUP) - heads


def prepare(lengths, points, peers, pair_count):
    rows = lengths.shape[0]
    body, _, extra = layout(points)
    return pl.pallas_call(
        functools.partial(prepare_kernel, peers, pair_count, points),
        out_shape=jax.ShapeDtypeStruct((rows, 2, sum(table_rows(peers, pair_count)), body + extra + 128), F32),
        in_specs=[pl.BlockSpec(memory_space=pltpu.VMEM)],
        out_specs=pl.BlockSpec(memory_space=pltpu.VMEM),
        compiler_params=pltpu.CompilerParams(vmem_limit_bytes=VMEM),
        cost_estimate=micros(1),
        name="prepare",
    )(lengths)


def fourier_kernel(groups, first_group, peers, pair_count, factor, mine, theirs, *refs):
    outs = refs[:peers]
    rows = factor.shape[0]
    scratch = refs[peers:]
    points = theirs.shape[0] // rows
    width = mine.shape[1]
    body, rest, extra = layout(points)
    tail, _ = table_rows(peers, pair_count)
    last_at = GROUP + peers
    set_index = lax.axis_index("set")
    sub = lax.broadcasted_iota(jnp.int32, (GROUP, 1), 0)
    whole = lax.broadcasted_iota(jnp.int32, (1, extra), 1) < 2 * rest
    size = 4 * GROUP * groups
    for r in range(rows):
        values, table, sums, twist = scratch[4 * r:4 * r + 4]
        length = factor[r, 0, tail - 1:tail, :width]
        for side, block in enumerate((mine, theirs)):
            store_values(values, side, row_of(block, r, rows, points), (set_index ^ side) * points, length)
        near = factor[r, 0, :GROUP, :], factor[r, 1, :GROUP, :]
        last = factor[r, 0, last_at:last_at + 1, :], factor[r, 1, last_at:last_at + 1, :]
        for peer in range(peers):
            at = GROUP + peer
            head = factor[r, 0, at:at + 1, :], factor[r, 1, at:at + 1, :]
            for g in range(groups):
                at = tail + first_group + g
                base = rotate(head, (factor[r, 0, at:at + 1, :], factor[r, 1, at:at + 1, :]))
                first = rotate(base, near)
                second = rotate(last, (first[0], -first[1]))
                block = jnp.concatenate([*first, *second], axis=0)
                lines = slice(peer * size + g * 4 * GROUP, peer * size + (g + 1) * 4 * GROUP)
                high, low = split(block[:, :body])
                for part, piece in enumerate((high, high, low)):
                    table[lines, part * body:(part + 1) * body] = piece
                if rest:
                    end = block[:, body:body + extra]
                    end = jnp.where(whole, end, end - end.astype(BF16).astype(F32))
                    table[lines, 3 * body:] = end.astype(BF16)
                twist[lines, :] = block[:, body + extra:]
        sums[...] = jnp.dot(table[...], values[...], preferred_element_type=F32)
    for r in range(rows):
        values, table, sums, twist = scratch[4 * r:4 * r + 4]
        length = factor[r, 0, tail - 1:tail, :width]
        for peer in range(peers):
            for g in range(groups):
                base = (set_index ^ (2 * peer)) * pair_count + (first_group + g) * GROUP
                for side in range(2):
                    wave = base + sub
                    wave = TRUNC - wave if side else wave
                    usable = (2 * wave + 1).astype(F32) <= length
                    at = ((peer * groups + g) * 2 + side) * 2 * GROUP
                    real, imag = slice(at, at + GROUP), slice(at + GROUP, at + 2 * GROUP)
                    far = rotate((twist[real, :], twist[imag, :]), (sums[real, width:], sums[imag, width:]))
                    for e, lines in enumerate((real, imag)):
                        to = (((g * 2 + side) * 2 + e) * rows + r) * GROUP
                        outs[peer][to:to + GROUP, :] = jnp.where(usable, sums[lines, :width] + far[e], 0.0)


def fourier_sums(factor, mine, theirs, groups, first_group, peers, pair_count):
    rows = factor.shape[0]
    width = mine.shape[1]
    body, _, extra = layout(theirs.shape[0] // rows)
    out_rows = groups * 4 * rows * GROUP
    tall = peers * groups * 4 * GROUP
    vmem = pl.BlockSpec(memory_space=pltpu.VMEM)
    return pl.pallas_call(
        functools.partial(fourier_kernel, groups, first_group, peers, pair_count),
        out_shape=[jax.ShapeDtypeStruct((out_rows, width), F32)] * peers,
        in_specs=[vmem] * 3,
        out_specs=[vmem] * peers,
        scratch_shapes=[
            pltpu.VMEM((3 * body + extra, 2 * width), BF16),
            pltpu.VMEM((tall, 3 * body + extra), BF16),
            pltpu.VMEM((tall, 2 * width), F32),
            pltpu.VMEM((tall, 128), F32),
        ] * rows,
        compiler_params=pltpu.CompilerParams(vmem_limit_bytes=VMEM),
        cost_estimate=micros(3),
        name="fourier_sums",
    )(factor, mine, theirs)


def weights_kernel(rows, bands, legend, out):
    pair_count, total, slots = legend.shape
    wide = out.shape[2]
    band_index = lax.axis_index("band")
    first_pair = lax.axis_index("set") * pair_count
    source = lax.broadcasted_iota(jnp.int32, (GROUP * total, 1), 0)
    lane = lax.broadcasted_iota(jnp.int32, (1, wide), 1)
    member = lane % GROUP
    row = lane // GROUP % rows
    parity = lane // (GROUP * rows) % 2
    side = lane // (GROUP * rows * 2) % 2
    band = (lane // (GROUP * rows * 4)) ^ band_index
    spread = (source == member * total + band * rows + row).astype(F32).astype(BF16)
    slot = band_index * slots + lax.broadcasted_iota(jnp.int32, (slots, 1), 0)
    for group in range(out.shape[0]):
        count = min(GROUP, pair_count - group * GROUP)
        held = legend[group * GROUP:group * GROUP + count].astype(F32).reshape(count * total, slots)
        if count < GROUP:
            held = jnp.concatenate([held, jnp.zeros(((GROUP - count) * total, slots), F32)], axis=0)
        moved = lax.dot_general(
            held.astype(BF16), spread, (((0,), (0,)), ((), ())), preferred_element_type=F32
        )
        first = TRUNC - (first_pair + group * GROUP + member)
        start = jnp.where(side == 0, 0, first + 1)
        sign = 1 - 2 * side
        match = (((slot - start) & 1) == parity) & (sign * slot <= sign * first - side)
        out[group] = jnp.where(match, moved, 0.0).astype(BF16)


def spread_weights(legend, rows, bands):
    pair_count, total, slots = legend.shape
    groups = pl.cdiv(pair_count, GROUP)
    vmem = pl.BlockSpec(memory_space=pltpu.VMEM)
    return pl.pallas_call(
        functools.partial(weights_kernel, rows, bands),
        out_shape=jax.ShapeDtypeStruct((groups, slots, bands * 4 * rows * GROUP), BF16),
        in_specs=[vmem],
        out_specs=vmem,
        compiler_params=pltpu.CompilerParams(vmem_limit_bytes=VMEM),
        cost_estimate=micros(1),
        name="spread_weights",
    )(legend)


def arrange(block):
    width = block.shape[1]
    tall = block.shape[0] // 4
    north = lax.broadcasted_iota(jnp.int32, (1, width), 1) < width // 2
    done = []
    for side in range(2):
        real = block[2 * side * tall:(2 * side + 1) * tall, :].astype(F32)
        imag = block[(2 * side + 1) * tall:(2 * side + 2) * tall, :].astype(F32)
        done.append(jnp.where(north, real, pltpu.roll(imag, width // 2, 1)))
        done.append(jnp.where(north, pltpu.roll(real, width // 2, 1), imag))
    return jnp.concatenate(done, axis=0).astype(BF16)


def spectra_kernel(bands, first_group, pairs, weights, *refs):
    held = refs[:bands]
    out, block, sems = refs[-3:]
    width = held[0].shape[1]
    tall = held[0].shape[0]
    groups = pl.cdiv(pairs, GROUP)
    part = tall // groups
    member = lax.broadcasted_iota(jnp.int32, (2 * GROUP, width), 0) % GROUP
    masks = [jnp.tile((member == i).astype(F32).astype(BF16), (bands * part // (2 * GROUP), 1)) for i in range(GROUP)]
    copies = []
    for g in range(groups):
        stacked = jnp.concatenate([arrange(ref[g * part:(g + 1) * part, :]) for ref in held], axis=0)
        for at in range(0, min(GROUP, pairs - g * GROUP), 2):
            both = jnp.concatenate([stacked * masks[at], stacked * masks[at + 1]], axis=1)
            product = jnp.dot(weights[first_group + g], both, preferred_element_type=F32)
            pair = g * GROUP + at
            block[pair] = product[:, :width]
            block[pair + 1] = product[:, width:]
            copy = pltpu.make_async_copy(
                block.at[pl.ds(pair, 2)], out.at[pl.ds(first_group * GROUP + pair, 2)], sems.at[pair // 2]
            )
            copy.start()
            copies.append(copy)
    for copy in copies:
        copy.wait()


def spectra_part(weights, held, out, pair_count, first_group, groups):
    bands = len(held)
    width = held[0].shape[1]
    slots = weights.shape[1]
    pairs = min(groups * GROUP, pair_count - first_group * GROUP)
    previous = [] if out is None else [out]
    vmem = pl.BlockSpec(memory_space=pltpu.VMEM)
    anywhere = pl.BlockSpec(memory_space=pl.ANY)
    return pl.pallas_call(
        functools.partial(spectra_kernel, bands, first_group, pairs),
        out_shape=jax.ShapeDtypeStruct((pair_count, slots, width), F32),
        in_specs=[vmem] * (1 + bands) + [anywhere] * len(previous),
        out_specs=anywhere,
        input_output_aliases={1 + bands: 0} if previous else {},
        scratch_shapes=[pltpu.VMEM((pairs, slots, width), F32), pltpu.SemaphoreType.DMA((pairs // 2,))],
        compiler_params=pltpu.CompilerParams(vmem_limit_bytes=VMEM),
        cost_estimate=micros(3),
        name="spectra_part",
    )(weights, *held, *previous)


def swap(axis, size, step):
    return [(i, i ^ step) for i in range(size)]


def exchange(array, axis, steps):
    return [lax.ppermute(part, axis, swap(axis, lax.axis_size(axis), step)) for part, step in zip(array, steps)]


def shards(grid, row_points, legendre):
    set_size = lax.axis_size("set")
    band_size = lax.axis_size("band")
    rows, points, width = grid.shape
    pair_count = legendre.shape[0]
    slots = legendre.shape[2] // band_size
    peers = set_size // 2
    flat = grid.transpose(1, 0, 2).reshape(points * rows, width)
    theirs = lax.ppermute(flat, "set", swap("set", set_size, 1))
    lengths = jnp.broadcast_to(row_points.astype(F32)[:, None], (rows, width))
    mine = flat
    factor = prepare(lengths, points, peers, pair_count)
    legend = lax.dynamic_slice_in_dim(legendre, lax.axis_index("band") * slots, slots, 2)
    legend, theirs = lax.optimization_barrier((legend, theirs))
    weights = None
    all_groups = pl.cdiv(pair_count, GROUP)
    cut = (all_groups + 1) // 2
    chunks = ((0, cut), (cut, all_groups - cut))
    gathered = []
    partial = []
    for first_group, groups in chunks:
        partial.append(fourier_sums(factor, mine, theirs, groups, first_group, peers, pair_count))
    for parts in partial:
        steps = list(range(1, peers))
        steps = steps[::-1] if gathered else steps[::2] + steps[1::2]
        arrived = exchange([parts[k].astype(WIRE) for k in steps], "set", [2 * k for k in steps])
        if gathered:
            legend, arrived[-1] = lax.optimization_barrier((legend, arrived[-1]))
            weights = spread_weights(legend, rows, band_size)
            arrived, weights = lax.optimization_barrier((arrived, weights))
        total = parts[0]
        for part in arrived:
            total = total + part.astype(F32)
        rounded = total.astype(BF16)
        turns = list(range(1, band_size))
        gathered.append([rounded] + exchange([rounded] * len(turns), "band", turns))
    out = None
    for held, (first_group, groups) in zip(gathered, chunks):
        out = spectra_part(weights, held, out, pair_count, first_group, groups)
    return out


def solution(mesh):
    return jax.shard_map(
        shards,
        mesh=mesh,
        in_specs=(P("band", "set", None), P("band"), P("set", None, None)),
        out_specs=P("set", "band", None),
        check_vma=False,
    )
```

```python
import functools
import math

import jax
import jax.numpy as jnp
from jax import lax
from jax.experimental import pallas as pl
from jax.experimental.pallas import tpu as pltpu
from jax.sharding import PartitionSpec as P

TRUNC = 1279
GROUP = 8
F32 = jnp.float32
BF16 = jnp.bfloat16
WIRE = jnp.float16
VMEM = 16 * 2**20


def round_up(value, step):
    return -(-value // step) * step


def unit_circle(multiplier, point, length, inverse):
    product = (multiplier * point).astype(F32)
    residue = product - jnp.floor(product * inverse + 0.5) * length
    quarters = 4.0 * residue * inverse
    turn = jnp.floor(quarters + 0.5)
    angle = (quarters - turn) * (0.5 * math.pi)
    square = angle * angle
    sine = angle * (1.0 + square * (-1 / 6 + square * (1 / 120 + square * (-1 / 5040 + square / 362880))))
    cosine = 1.0 + square * (-0.5 + square * (1 / 24 + square * (-1 / 720 + square / 40320)))
    quadrant = turn.astype(jnp.int32) & 3
    odd = (quadrant & 1) == 1
    real = jnp.where(odd, sine, cosine)
    imag = jnp.where(odd, cosine, sine)
    real = jnp.where((quadrant == 1) | (quadrant == 2), -real, real)
    imag = jnp.where(quadrant >= 2, imag, -imag)
    return real, imag


def micros(count):
    return pl.CostEstimate(flops=0, bytes_accessed=count * 3 * 10**6, transcendentals=0)


def rotate(a, b):
    return a[0] * b[0] - a[1] * b[1], a[0] * b[1] + a[1] * b[0]


def split(values):
    high = values.astype(BF16)
    return high, (values - high.astype(F32)).astype(BF16)


def layout(points):
    rest = points % 128
    return points - rest, rest, round_up(3 * rest, 128)


def hemisphere_sign(width):
    return jnp.where(lax.broadcasted_iota(jnp.int32, (1, width), 1) < width // 2, 1.0, -1.0)


def store_values(out, side, raw, start, length):
    points, width = raw.shape
    body, rest, extra = layout(points)
    sign = hemisphere_sign(width)
    where = start + lax.broadcasted_iota(jnp.int32, (points, 1), 0)
    folded = pltpu.roll(raw, width // 2, 1) + raw * sign
    folded = jnp.where(where.astype(F32) < length, folded, 0.0)
    lanes = slice(side * width, (side + 1) * width)
    high, low = split(folded[:body])
    for part, piece in enumerate((high, low, high)):
        out[part * body:(part + 1) * body, lanes] = piece
    if rest:
        high, low = split(folded[body:])
        parts = [piece.astype(F32) for piece in (high, low, high)]
        parts.append(jnp.zeros((extra - 3 * rest, width), F32))
        out[3 * body:, lanes] = jnp.concatenate(parts, axis=0).astype(BF16)


def row_of(block, r, rows, points):
    return block[pl.ds(r, points, stride=rows), :]


def prepare_kernel(peers, pair_count, points, lengths, factor):
    rows, _, tall, wide = factor.shape
    body, rest, extra = layout(points)
    set_index = lax.axis_index("set")
    start = set_index * points
    beside = (set_index ^ 1) * points - start
    slot = lax.broadcasted_iota(jnp.int32, (1, wide), 1)
    point = start + jnp.where(slot < body, slot, body + (slot - body) % max(rest, 1))
    point = jnp.where(slot < body + extra, point, beside)
    heads = peers + 2
    sub = lax.broadcasted_iota(jnp.int32, (tall, 1), 0)
    order = sub - GROUP
    head = jnp.where(order < peers, (set_index ^ (2 * order)) * pair_count, TRUNC)
    multiplier = jnp.where(sub < GROUP, sub, jnp.where(order < heads, head, (order - heads) * GROUP))
    for r in range(rows):
        length = lengths[r:r + 1, :1]
        scale = jnp.where(slot < body + extra, lax.rsqrt(jnp.broadcast_to(length, (1, wide))) * headroom(points), 1.0)
        scale = jnp.where(sub < GROUP, scale, 1.0)
        real, imag = unit_circle(multiplier, point, length, 1.0 / length)
        factor[r, 0] = jnp.where(order == heads - 1, length, real * scale)
        factor[r, 1] = imag * scale


def headroom(points):
    return 2.0 ** math.floor(math.log2(60000 / (12 * math.sqrt(2 * points))))


def table_rows(peers, pair_count):
    heads, groups = peers + 2, pl.cdiv(pair_count, GROUP)
    return GROUP + heads, round_up(heads + groups, GROUP) - heads


def prepare(lengths, points, peers, pair_count):
    rows = lengths.shape[0]
    body, _, extra = layout(points)
    return pl.pallas_call(
        functools.partial(prepare_kernel, peers, pair_count, points),
        out_shape=jax.ShapeDtypeStruct((rows, 2, sum(table_rows(peers, pair_count)), body + extra + 128), F32),
        in_specs=[pl.BlockSpec(memory_space=pltpu.VMEM)],
        out_specs=pl.BlockSpec(memory_space=pltpu.VMEM),
        compiler_params=pltpu.CompilerParams(vmem_limit_bytes=VMEM),
        cost_estimate=micros(1),
        name="prepare",
    )(lengths)


def fourier_kernel(groups, first_group, peers, pair_count, factor, mine, theirs, *refs):
    outs = refs[:peers]
    rows = factor.shape[0]
    scratch = refs[peers:]
    points = theirs.shape[0] // rows
    width = mine.shape[1]
    body, rest, extra = layout(points)
    tail, _ = table_rows(peers, pair_count)
    last_at = GROUP + peers
    set_index = lax.axis_index("set")
    sub = lax.broadcasted_iota(jnp.int32, (GROUP, 1), 0)
    whole = lax.broadcasted_iota(jnp.int32, (1, extra), 1) < 2 * rest
    size = 4 * GROUP * groups
    for r in range(rows):
        values, table, sums, twist = scratch[4 * r:4 * r + 4]
        length = factor[r, 0, tail - 1:tail, :width]
        for side, block in enumerate((mine, theirs)):
            store_values(values, side, row_of(block, r, rows, points), (set_index ^ side) * points, length)
        near = factor[r, 0, :GROUP, :], factor[r, 1, :GROUP, :]
        last = factor[r, 0, last_at:last_at + 1, :], factor[r, 1, last_at:last_at + 1, :]
        for peer in range(peers):
            at = GROUP + peer
            head = factor[r, 0, at:at + 1, :], factor[r, 1, at:at + 1, :]
            for g in range(groups):
                at = tail + first_group + g
                base = rotate(head, (factor[r, 0, at:at + 1, :], factor[r, 1, at:at + 1, :]))
                first = rotate(base, near)
                second = rotate(last, (first[0], -first[1]))
                block = jnp.concatenate([*first, *second], axis=0)
                lines = slice(peer * size + g * 4 * GROUP, peer * size + (g + 1) * 4 * GROUP)
                high, low = split(block[:, :body])
                for part, piece in enumerate((high, high, low)):
                    table[lines, part * body:(part + 1) * body] = piece
                if rest:
                    end = block[:, body:body + extra]
                    end = jnp.where(whole, end, end - end.astype(BF16).astype(F32))
                    table[lines, 3 * body:] = end.astype(BF16)
                twist[lines, :] = block[:, body + extra:]
        sums[...] = jnp.dot(table[...], values[...], preferred_element_type=F32)
    for r in range(rows):
        values, table, sums, twist = scratch[4 * r:4 * r + 4]
        length = factor[r, 0, tail - 1:tail, :width]
        for peer in range(peers):
            for g in range(groups):
                base = (set_index ^ (2 * peer)) * pair_count + (first_group + g) * GROUP
                for side in range(2):
                    wave = base + sub
                    wave = TRUNC - wave if side else wave
                    usable = (2 * wave + 1).astype(F32) <= length
                    at = ((peer * groups + g) * 2 + side) * 2 * GROUP
                    real, imag = slice(at, at + GROUP), slice(at + GROUP, at + 2 * GROUP)
                    far = rotate((twist[real, :], twist[imag, :]), (sums[real, width:], sums[imag, width:]))
                    for e, lines in enumerate((real, imag)):
                        to = (((g * 2 + side) * 2 + e) * rows + r) * GROUP
                        outs[peer][to:to + GROUP, :] = jnp.where(usable, sums[lines, :width] + far[e], 0.0)


def fourier_sums(factor, mine, theirs, groups, first_group, peers, pair_count):
    rows = factor.shape[0]
    width = mine.shape[1]
    body, _, extra = layout(theirs.shape[0] // rows)
    out_rows = groups * 4 * rows * GROUP
    tall = peers * groups * 4 * GROUP
    vmem = pl.BlockSpec(memory_space=pltpu.VMEM)
    return pl.pallas_call(
        functools.partial(fourier_kernel, groups, first_group, peers, pair_count),
        out_shape=[jax.ShapeDtypeStruct((out_rows, width), F32)] * peers,
        in_specs=[vmem] * 3,
        out_specs=[vmem] * peers,
        scratch_shapes=[
            pltpu.VMEM((3 * body + extra, 2 * width), BF16),
            pltpu.VMEM((tall, 3 * body + extra), BF16),
            pltpu.VMEM((tall, 2 * width), F32),
            pltpu.VMEM((tall, 128), F32),
        ] * rows,
        compiler_params=pltpu.CompilerParams(vmem_limit_bytes=VMEM),
        cost_estimate=micros(3),
        name="fourier_sums",
    )(factor, mine, theirs)


def weights_kernel(rows, bands, legend, out):
    pair_count, total, slots = legend.shape
    wide = out.shape[2]
    band_index = lax.axis_index("band")
    first_pair = lax.axis_index("set") * pair_count
    source = lax.broadcasted_iota(jnp.int32, (GROUP * total, 1), 0)
    lane = lax.broadcasted_iota(jnp.int32, (1, wide), 1)
    member = lane % GROUP
    row = lane // GROUP % rows
    parity = lane // (GROUP * rows) % 2
    side = lane // (GROUP * rows * 2) % 2
    band = (lane // (GROUP * rows * 4)) ^ band_index
    spread = (source == member * total + band * rows + row).astype(F32).astype(BF16)
    slot = band_index * slots + lax.broadcasted_iota(jnp.int32, (slots, 1), 0)
    for group in range(out.shape[0]):
        count = min(GROUP, pair_count - group * GROUP)
        held = legend[group * GROUP:group * GROUP + count].astype(F32).reshape(count * total, slots)
        if count < GROUP:
            held = jnp.concatenate([held, jnp.zeros(((GROUP - count) * total, slots), F32)], axis=0)
        moved = lax.dot_general(
            held.astype(BF16), spread, (((0,), (0,)), ((), ())), preferred_element_type=F32
        )
        first = TRUNC - (first_pair + group * GROUP + member)
        start = jnp.where(side == 0, 0, first + 1)
        sign = 1 - 2 * side
        match = (((slot - start) & 1) == parity) & (sign * slot <= sign * first - side)
        out[group] = jnp.where(match, moved, 0.0).astype(BF16)


def spread_weights(legend, rows, bands):
    pair_count, total, slots = legend.shape
    groups = pl.cdiv(pair_count, GROUP)
    vmem = pl.BlockSpec(memory_space=pltpu.VMEM)
    return pl.pallas_call(
        functools.partial(weights_kernel, rows, bands),
        out_shape=jax.ShapeDtypeStruct((groups, slots, bands * 4 * rows * GROUP), BF16),
        in_specs=[vmem],
        out_specs=vmem,
        compiler_params=pltpu.CompilerParams(vmem_limit_bytes=VMEM),
        cost_estimate=micros(1),
        name="spread_weights",
    )(legend)


def arrange(block):
    width = block.shape[1]
    tall = block.shape[0] // 4
    north = lax.broadcasted_iota(jnp.int32, (1, width), 1) < width // 2
    done = []
    for side in range(2):
        real = block[2 * side * tall:(2 * side + 1) * tall, :].astype(F32)
        imag = block[(2 * side + 1) * tall:(2 * side + 2) * tall, :].astype(F32)
        done.append(jnp.where(north, real, pltpu.roll(imag, width // 2, 1)))
        done.append(jnp.where(north, pltpu.roll(real, width // 2, 1), imag))
    return jnp.concatenate(done, axis=0).astype(BF16)


def spectra_kernel(bands, first_group, pairs, weights, *refs):
    held = refs[:bands]
    out, block, sems = refs[-3:]
    width = held[0].shape[1]
    tall = held[0].shape[0]
    groups = pl.cdiv(pairs, GROUP)
    part = tall // groups
    member = lax.broadcasted_iota(jnp.int32, (2 * GROUP, width), 0) % GROUP
    masks = [jnp.tile((member == i).astype(F32).astype(BF16), (bands * part // (2 * GROUP), 1)) for i in range(GROUP)]
    copies = []
    for g in range(groups):
        stacked = jnp.concatenate([arrange(ref[g * part:(g + 1) * part, :]) for ref in held], axis=0)
        for at in range(0, min(GROUP, pairs - g * GROUP), 2):
            both = jnp.concatenate([stacked * masks[at], stacked * masks[at + 1]], axis=1)
            product = jnp.dot(weights[first_group + g], both, preferred_element_type=F32)
            pair = g * GROUP + at
            block[pair] = product[:, :width]
            block[pair + 1] = product[:, width:]
            copy = pltpu.make_async_copy(
                block.at[pl.ds(pair, 2)], out.at[pl.ds(first_group * GROUP + pair, 2)], sems.at[pair // 2]
            )
            copy.start()
            copies.append(copy)
    for copy in copies:
        copy.wait()


def spectra_part(weights, held, out, pair_count, first_group, groups):
    bands = len(held)
    width = held[0].shape[1]
    slots = weights.shape[1]
    pairs = min(groups * GROUP, pair_count - first_group * GROUP)
    previous = [] if out is None else [out]
    vmem = pl.BlockSpec(memory_space=pltpu.VMEM)
    anywhere = pl.BlockSpec(memory_space=pl.ANY)
    return pl.pallas_call(
        functools.partial(spectra_kernel, bands, first_group, pairs),
        out_shape=jax.ShapeDtypeStruct((pair_count, slots, width), F32),
        in_specs=[vmem] * (1 + bands) + [anywhere] * len(previous),
        out_specs=anywhere,
        input_output_aliases={1 + bands: 0} if previous else {},
        scratch_shapes=[pltpu.VMEM((pairs, slots, width), F32), pltpu.SemaphoreType.DMA((pairs // 2,))],
        compiler_params=pltpu.CompilerParams(vmem_limit_bytes=VMEM),
        cost_estimate=micros(3),
        name="spectra_part",
    )(weights, *held, *previous)


def swap(axis, size, step):
    return [(i, i ^ step) for i in range(size)]


def exchange(array, axis, steps):
    return [lax.ppermute(part, axis, swap(axis, lax.axis_size(axis), step)) for part, step in zip(array, steps)]


def shards(grid, row_points, legendre):
    set_size = lax.axis_size("set")
    band_size = lax.axis_size("band")
    rows, points, width = grid.shape
    pair_count = legendre.shape[0]
    slots = legendre.shape[2] // band_size
    peers = set_size // 2
    flat = grid.transpose(1, 0, 2).reshape(points * rows, width)
    theirs = lax.ppermute(flat, "set", swap("set", set_size, 1))
    lengths = jnp.broadcast_to(row_points.astype(F32)[:, None], (rows, width))
    mine = flat
    factor = prepare(lengths, points, peers, pair_count)
    legend = lax.dynamic_slice_in_dim(legendre, lax.axis_index("band") * slots, slots, 2)
    legend, theirs = lax.optimization_barrier((legend, theirs))
    weights = None
    all_groups = pl.cdiv(pair_count, GROUP)
    cut = (all_groups + 1) // 2
    chunks = ((0, cut), (cut, all_groups - cut))
    gathered = []
    partial = []
    for first_group, groups in chunks:
        partial.append(fourier_sums(factor, mine, theirs, groups, first_group, peers, pair_count))
    for parts in partial:
        steps = list(range(1, peers))
        steps = steps[::-1] if gathered else steps[::2] + steps[1::2]
        arrived = exchange([parts[k].astype(WIRE) for k in steps], "set", [2 * k for k in steps])
        if gathered:
            legend, arrived[-1] = lax.optimization_barrier((legend, arrived[-1]))
            weights = spread_weights(legend, rows, band_size)
            arrived, weights = lax.optimization_barrier((arrived, weights))
        total = parts[0]
        for part in arrived:
            total = total + part.astype(F32)
        rounded = (total * (1 / headroom(points))).astype(BF16)
        turns = list(range(1, band_size))
        gathered.append([rounded] + exchange([rounded] * len(turns), "band", turns))
    out = None
    for held, (first_group, groups) in zip(gathered, chunks):
        out = spectra_part(weights, held, out, pair_count, first_group, groups)
    return out


def solution(mesh):
    return jax.shard_map(
        shards,
        mesh=mesh,
        in_specs=(P("band", "set", None), P("band"), P("set", None, None)),
        out_specs=P("set", "band", None),
        check_vma=False,
    )
```

```python
import functools
import math

import jax
import jax.numpy as jnp
from jax import lax
from jax.experimental import pallas as pl
from jax.experimental.pallas import tpu as pltpu
from jax.sharding import PartitionSpec as P

TRUNC = 1279
GROUP = 8
F32 = jnp.float32
BF16 = jnp.bfloat16
WIRE = jnp.float16
VMEM = 16 * 2**20


def round_up(value, step):
    return -(-value // step) * step


def unit_circle(multiplier, point, length, inverse):
    product = (multiplier * point).astype(F32)
    residue = product - jnp.floor(product * inverse + 0.5) * length
    quarters = 4.0 * residue * inverse
    turn = jnp.floor(quarters + 0.5)
    angle = (quarters - turn) * (0.5 * math.pi)
    square = angle * angle
    sine = angle * (1.0 + square * (-1 / 6 + square * (1 / 120 + square * (-1 / 5040 + square / 362880))))
    cosine = 1.0 + square * (-0.5 + square * (1 / 24 + square * (-1 / 720 + square / 40320)))
    quadrant = turn.astype(jnp.int32) & 3
    odd = (quadrant & 1) == 1
    real = jnp.where(odd, sine, cosine)
    imag = jnp.where(odd, cosine, sine)
    real = jnp.where((quadrant == 1) | (quadrant == 2), -real, real)
    imag = jnp.where(quadrant >= 2, imag, -imag)
    return real, imag


def micros(count):
    return pl.CostEstimate(flops=0, bytes_accessed=count * 3 * 10**6, transcendentals=0)


def rotate(a, b):
    return a[0] * b[0] - a[1] * b[1], a[0] * b[1] + a[1] * b[0]


def split(values):
    high = values.astype(BF16)
    return high, (values - high.astype(F32)).astype(BF16)


def layout(points):
    rest = points % 128
    return points - rest, rest, round_up(3 * rest, 128)


def hemisphere_sign(width):
    return jnp.where(lax.broadcasted_iota(jnp.int32, (1, width), 1) < width // 2, 1.0, -1.0)


def store_values(out, side, raw, start, length):
    points, width = raw.shape
    body, rest, extra = layout(points)
    sign = hemisphere_sign(width)
    where = start + lax.broadcasted_iota(jnp.int32, (points, 1), 0)
    folded = pltpu.roll(raw, width // 2, 1) + raw * sign
    folded = jnp.where(where.astype(F32) < length, folded, 0.0)
    lanes = slice(side * width, (side + 1) * width)
    high, low = split(folded[:body])
    for part, piece in enumerate((high, low, high)):
        out[part * body:(part + 1) * body, lanes] = piece
    if rest:
        high, low = split(folded[body:])
        parts = [piece.astype(F32) for piece in (high, low, high)]
        parts.append(jnp.zeros((extra - 3 * rest, width), F32))
        out[3 * body:, lanes] = jnp.concatenate(parts, axis=0).astype(BF16)


def row_of(block, r, rows, points):
    return block[pl.ds(r, points, stride=rows), :]


def prepare_kernel(peers, pair_count, points, lengths, factor):
    rows, _, tall, wide = factor.shape
    body, rest, extra = layout(points)
    set_index = lax.axis_index("set")
    start = set_index * points
    beside = (set_index ^ 1) * points - start
    slot = lax.broadcasted_iota(jnp.int32, (1, wide), 1)
    point = start + jnp.where(slot < body, slot, body + (slot - body) % max(rest, 1))
    point = jnp.where(slot < body + extra, point, beside)
    heads = peers + 2
    sub = lax.broadcasted_iota(jnp.int32, (tall, 1), 0)
    order = sub - GROUP
    head = jnp.where(order < peers, (set_index ^ (2 * order)) * pair_count, TRUNC)
    multiplier = jnp.where(sub < GROUP, sub, jnp.where(order < heads, head, (order - heads) * GROUP))
    for r in range(rows):
        length = lengths[r:r + 1, :1]
        scale = jnp.where(slot < body + extra, lax.rsqrt(jnp.broadcast_to(length, (1, wide))) * headroom(points), 1.0)
        scale = jnp.where(sub < GROUP, scale, 1.0)
        real, imag = unit_circle(multiplier, point, length, 1.0 / length)
        factor[r, 0] = jnp.where(order == heads - 1, length, real * scale)
        factor[r, 1] = imag * scale


def headroom(points):
    return 2.0 ** math.floor(math.log2(60000 / (12 * math.sqrt(2 * points))))


def table_rows(peers, pair_count):
    heads, groups = peers + 2, pl.cdiv(pair_count, GROUP)
    return GROUP + heads, round_up(heads + groups, GROUP) - heads


def prepare(lengths, points, peers, pair_count):
    rows = lengths.shape[0]
    body, _, extra = layout(points)
    return pl.pallas_call(
        functools.partial(prepare_kernel, peers, pair_count, points),
        out_shape=jax.ShapeDtypeStruct((rows, 2, sum(table_rows(peers, pair_count)), body + extra + 128), F32),
        in_specs=[pl.BlockSpec(memory_space=pltpu.VMEM)],
        out_specs=pl.BlockSpec(memory_space=pltpu.VMEM),
        compiler_params=pltpu.CompilerParams(vmem_limit_bytes=VMEM),
        cost_estimate=micros(1),
        name="prepare",
    )(lengths)


def fourier_kernel(groups, first_group, peers, pair_count, factor, mine, theirs, *refs):
    outs = refs[:peers]
    rows = factor.shape[0]
    scratch = refs[peers:]
    points = theirs.shape[0] // rows
    width = mine.shape[1]
    body, rest, extra = layout(points)
    tail, _ = table_rows(peers, pair_count)
    last_at = GROUP + peers
    set_index = lax.axis_index("set")
    sub = lax.broadcasted_iota(jnp.int32, (GROUP, 1), 0)
    whole = lax.broadcasted_iota(jnp.int32, (1, extra), 1) < 2 * rest
    size = 4 * GROUP * groups
    for r in range(rows):
        values, table, sums, twist = scratch[4 * r:4 * r + 4]
        length = factor[r, 0, tail - 1:tail, :width]
        for side, block in enumerate((mine, theirs)):
            store_values(values, side, row_of(block, r, rows, points), (set_index ^ side) * points, length)
        near = factor[r, 0, :GROUP, :], factor[r, 1, :GROUP, :]
        last = factor[r, 0, last_at:last_at + 1, :], factor[r, 1, last_at:last_at + 1, :]
        for peer in range(peers):
            at = GROUP + peer
            head = factor[r, 0, at:at + 1, :], factor[r, 1, at:at + 1, :]
            for g in range(groups):
                at = tail + first_group + g
                base = rotate(head, (factor[r, 0, at:at + 1, :], factor[r, 1, at:at + 1, :]))
                first = rotate(base, near)
                second = rotate(last, (first[0], -first[1]))
                block = jnp.concatenate([*first, *second], axis=0)
                lines = slice(peer * size + g * 4 * GROUP, peer * size + (g + 1) * 4 * GROUP)
                high, low = split(block[:, :body])
                for part, piece in enumerate((high, high, low)):
                    table[lines, part * body:(part + 1) * body] = piece
                if rest:
                    end = block[:, body:body + extra]
                    end = jnp.where(whole, end, end - end.astype(BF16).astype(F32))
                    table[lines, 3 * body:] = end.astype(BF16)
                twist[lines, :] = block[:, body + extra:]
        sums[...] = jnp.dot(table[...], values[...], preferred_element_type=F32)
    for r in range(rows):
        values, table, sums, twist = scratch[4 * r:4 * r + 4]
        length = factor[r, 0, tail - 1:tail, :width]
        for peer in range(peers):
            for g in range(groups):
                base = (set_index ^ (2 * peer)) * pair_count + (first_group + g) * GROUP
                for side in range(2):
                    wave = base + sub
                    wave = TRUNC - wave if side else wave
                    usable = (2 * wave + 1).astype(F32) <= length
                    at = ((peer * groups + g) * 2 + side) * 2 * GROUP
                    real, imag = slice(at, at + GROUP), slice(at + GROUP, at + 2 * GROUP)
                    far = rotate((twist[real, :], twist[imag, :]), (sums[real, width:], sums[imag, width:]))
                    for e, lines in enumerate((real, imag)):
                        to = (((g * 2 + side) * 2 + e) * rows + r) * GROUP
                        outs[peer][to:to + GROUP, :] = jnp.where(usable, sums[lines, :width] + far[e], 0.0)


def fourier_sums(factor, mine, theirs, groups, first_group, peers, pair_count):
    rows = factor.shape[0]
    width = mine.shape[1]
    body, _, extra = layout(theirs.shape[0] // rows)
    out_rows = groups * 4 * rows * GROUP
    tall = peers * groups * 4 * GROUP
    vmem = pl.BlockSpec(memory_space=pltpu.VMEM)
    return pl.pallas_call(
        functools.partial(fourier_kernel, groups, first_group, peers, pair_count),
        out_shape=[jax.ShapeDtypeStruct((out_rows, width), F32)] * peers,
        in_specs=[vmem] * 3,
        out_specs=[vmem] * peers,
        scratch_shapes=[
            pltpu.VMEM((3 * body + extra, 2 * width), BF16),
            pltpu.VMEM((tall, 3 * body + extra), BF16),
            pltpu.VMEM((tall, 2 * width), F32),
            pltpu.VMEM((tall, 128), F32),
        ] * rows,
        compiler_params=pltpu.CompilerParams(vmem_limit_bytes=VMEM),
        cost_estimate=micros(3),
        name="fourier_sums",
    )(factor, mine, theirs)


def weights_kernel(rows, bands, legend, out):
    pair_count, total, slots = legend.shape
    wide = out.shape[2]
    band_index = lax.axis_index("band")
    first_pair = lax.axis_index("set") * pair_count
    source = lax.broadcasted_iota(jnp.int32, (GROUP * total, 1), 0)
    lane = lax.broadcasted_iota(jnp.int32, (1, wide), 1)
    member = lane % GROUP
    row = lane // GROUP % rows
    parity = lane // (GROUP * rows) % 2
    side = lane // (GROUP * rows * 2) % 2
    band = (lane // (GROUP * rows * 4)) ^ band_index
    spread = (source == member * total + band * rows + row).astype(F32).astype(BF16)
    slot = band_index * slots + lax.broadcasted_iota(jnp.int32, (slots, 1), 0)
    for group in range(out.shape[0]):
        count = min(GROUP, pair_count - group * GROUP)
        held = legend[group * GROUP:group * GROUP + count].astype(F32).reshape(count * total, slots)
        if count < GROUP:
            held = jnp.concatenate([held, jnp.zeros(((GROUP - count) * total, slots), F32)], axis=0)
        moved = lax.dot_general(
            held.astype(BF16), spread, (((0,), (0,)), ((), ())), preferred_element_type=F32
        )
        first = TRUNC - (first_pair + group * GROUP + member)
        start = jnp.where(side == 0, 0, first + 1)
        sign = 1 - 2 * side
        match = (((slot - start) & 1) == parity) & (sign * slot <= sign * first - side)
        out[group] = jnp.where(match, moved, 0.0).astype(BF16)


def spread_weights(legend, rows, bands):
    pair_count, total, slots = legend.shape
    groups = pl.cdiv(pair_count, GROUP)
    vmem = pl.BlockSpec(memory_space=pltpu.VMEM)
    return pl.pallas_call(
        functools.partial(weights_kernel, rows, bands),
        out_shape=jax.ShapeDtypeStruct((groups, slots, bands * 4 * rows * GROUP), BF16),
        in_specs=[vmem],
        out_specs=vmem,
        compiler_params=pltpu.CompilerParams(vmem_limit_bytes=VMEM),
        cost_estimate=micros(1),
        name="spread_weights",
    )(legend)


def arrange(block):
    width = block.shape[1]
    tall = block.shape[0] // 4
    north = lax.broadcasted_iota(jnp.int32, (1, width), 1) < width // 2
    done = []
    for side in range(2):
        real = block[2 * side * tall:(2 * side + 1) * tall, :].astype(F32)
        imag = block[(2 * side + 1) * tall:(2 * side + 2) * tall, :].astype(F32)
        done.append(jnp.where(north, real, pltpu.roll(imag, width // 2, 1)))
        done.append(jnp.where(north, pltpu.roll(real, width // 2, 1), imag))
    return jnp.concatenate(done, axis=0).astype(BF16)


def spectra_kernel(bands, first_group, pairs, weights, *refs):
    held = refs[:bands]
    out, block, sems = refs[-3:]
    width = held[0].shape[1]
    tall = held[0].shape[0]
    groups = pl.cdiv(pairs, GROUP)
    part = tall // groups
    member = lax.broadcasted_iota(jnp.int32, (2 * GROUP, width), 0) % GROUP
    masks = [jnp.tile((member == i).astype(F32).astype(BF16), (bands * part // (2 * GROUP), 1)) for i in range(GROUP)]
    copies = []
    for g in range(groups):
        stacked = jnp.concatenate([arrange(ref[g * part:(g + 1) * part, :]) for ref in held], axis=0)
        for at in range(0, min(GROUP, pairs - g * GROUP), 2):
            both = jnp.concatenate([stacked * masks[at], stacked * masks[at + 1]], axis=1)
            product = jnp.dot(weights[first_group + g], both, preferred_element_type=F32)
            pair = g * GROUP + at
            block[pair] = product[:, :width]
            block[pair + 1] = product[:, width:]
            copy = pltpu.make_async_copy(
                block.at[pl.ds(pair, 2)], out.at[pl.ds(first_group * GROUP + pair, 2)], sems.at[pair // 2]
            )
            copy.start(priority=len(copies) % 2)
            copies.append(copy)
    for copy in copies:
        copy.wait()


def spectra_part(weights, held, out, pair_count, first_group, groups):
    bands = len(held)
    width = held[0].shape[1]
    slots = weights.shape[1]
    pairs = min(groups * GROUP, pair_count - first_group * GROUP)
    previous = [] if out is None else [out]
    vmem = pl.BlockSpec(memory_space=pltpu.VMEM)
    anywhere = pl.BlockSpec(memory_space=pl.ANY)
    return pl.pallas_call(
        functools.partial(spectra_kernel, bands, first_group, pairs),
        out_shape=jax.ShapeDtypeStruct((pair_count, slots, width), F32),
        in_specs=[vmem] * (1 + bands) + [anywhere] * len(previous),
        out_specs=anywhere,
        input_output_aliases={1 + bands: 0} if previous else {},
        scratch_shapes=[pltpu.VMEM((pairs, slots, width), F32), pltpu.SemaphoreType.DMA((pairs // 2,))],
        compiler_params=pltpu.CompilerParams(vmem_limit_bytes=VMEM),
        cost_estimate=micros(3),
        name="spectra_part",
    )(weights, *held, *previous)


def swap(axis, size, step):
    return [(i, i ^ step) for i in range(size)]


def exchange(array, axis, steps):
    return [lax.ppermute(part, axis, swap(axis, lax.axis_size(axis), step)) for part, step in zip(array, steps)]


def shards(grid, row_points, legendre):
    set_size = lax.axis_size("set")
    band_size = lax.axis_size("band")
    rows, points, width = grid.shape
    pair_count = legendre.shape[0]
    slots = legendre.shape[2] // band_size
    peers = set_size // 2
    flat = grid.transpose(1, 0, 2).reshape(points * rows, width)
    theirs = lax.ppermute(flat, "set", swap("set", set_size, 1))
    lengths = jnp.broadcast_to(row_points.astype(F32)[:, None], (rows, width))
    mine = flat
    factor = prepare(lengths, points, peers, pair_count)
    legend = lax.dynamic_slice_in_dim(legendre, lax.axis_index("band") * slots, slots, 2)
    legend, theirs = lax.optimization_barrier((legend, theirs))
    weights = None
    all_groups = pl.cdiv(pair_count, GROUP)
    cut = (all_groups + 1) // 2
    chunks = ((0, cut), (cut, all_groups - cut))
    gathered = []
    partial = []
    for first_group, groups in chunks:
        partial.append(fourier_sums(factor, mine, theirs, groups, first_group, peers, pair_count))
    for parts in partial:
        steps = list(range(1, peers))
        steps = steps[::-1] if gathered else steps[::2] + steps[1::2]
        arrived = exchange([parts[k].astype(WIRE) for k in steps], "set", [2 * k for k in steps])
        if gathered:
            legend, arrived[-1] = lax.optimization_barrier((legend, arrived[-1]))
            weights = spread_weights(legend, rows, band_size)
            arrived, weights = lax.optimization_barrier((arrived, weights))
        total = parts[0]
        for part in arrived:
            total = total + part.astype(F32)
        rounded = (total * (1 / headroom(points))).astype(BF16)
        turns = list(range(1, band_size))
        gathered.append([rounded] + exchange([rounded] * len(turns), "band", turns))
    out = None
    for held, (first_group, groups) in zip(gathered, chunks):
        out = spectra_part(weights, held, out, pair_count, first_group, groups)
    return out


def solution(mesh):
    return jax.shard_map(
        shards,
        mesh=mesh,
        in_specs=(P("band", "set", None), P("band"), P("set", None, None)),
        out_specs=P("set", "band", None),
        check_vma=False,
    )
```
